32 devices in a mesh: groups: 2 (over x), row: 8 (over z, y), col: 2 (over core).
Axes of the slice: x: 2, y: 2, z: 4, core: 2. Of those that a mesh axis runs over, the one named last changes fastest.
Arguments:
- pair_rep: bfloat16 [160, 80, 128], P(('groups', 'row'), 'col'), parts along dimension 0, as said below
- proj_weight: bfloat16 [128, 512], replicated, may hold values from -0.5 to 0.5
- gate_weight: bfloat16 [128, 128], replicated, may hold values from -0.5 to 0.5
- out_weight: bfloat16 [128, 128], replicated, may hold values from -0.5 to 0.5
Outputs:
- update: bfloat16 [160, 80, 128], P(('groups', 'row'), 'col'), parts along dimension 0
The draws below stay inside these ranges and needn't reach their ends.
There are 2 independent parts, one for each index of `groups`. The reference program is written for one: setup_inputs(seed, part) draws one part's arguments, and reference() takes and returns one part's arrays. A program takes and returns all parts, laid end to end along the dimension named above; an argument that names none is the same for every part. Nothing has to cross between parts.
Inputs may be any that keep to these rules, and one draw needn't show every extreme that they name: `pair_rep`: real-valued pair features; each pair position and each channel carries its own scale factor between 1 and 10.
All inputs are finite; a program needn't handle non-finite values.
Results may differ from the reference program's by a relative error of at most 0.0078.
Values may be sent and summed in bfloat16 or wider, within the bound.
No kernel may reach another device: no remote copies, remote signals or barrier semaphores. Data moves between devices by JAX's collectives and lax.ppermute only.
A program may use at most 128 MiB of HBM per device.

```python
import math
import jax
import jax.numpy as jnp
from jax import lax

C = 128
CH = 128
L = 80


def draw_pair_rep(key, part):
    first, second, third = jax.random.split(key, 3)
    position_scale = jnp.exp(jax.random.uniform(second, (L, L, 1), jnp.float32, 0.0, math.log(10.0)))
    channel_scale = jnp.exp(jax.random.uniform(third, (C,), jnp.float32, 0.0, math.log(10.0)))
    base = jax.random.normal(first, (L, L, C), jnp.float32)
    return (base * position_scale * channel_scale).astype(jnp.bfloat16)


def bell_draw(rng, dims, deviation, bound, kind=jnp.bfloat16):
    drawn = jax.random.normal(rng, dims, jnp.float32) * deviation
    return jnp.minimum(jnp.maximum(drawn, -bound), bound).astype(kind)


def setup_inputs(seed: int = 0, part: int = 0) -> dict:
    seeds = jax.random.split(jax.random.key(seed), 5)
    part_keys = jax.random.split(jax.random.fold_in(seeds[4], part), 5)
    pair_rep = draw_pair_rep(jax.random.fold_in(jax.random.fold_in(seeds[4], part), 71), part)
    proj_weight = bell_draw(seeds[1], (C, 4 * CH), C ** -0.5, 0.5)
    gate_weight = bell_draw(seeds[2], (C, C), C ** -0.5, 0.5)
    out_weight = bell_draw(seeds[3], (CH, C), CH ** -0.5, 0.5)
    return dict(pair_rep=pair_rep, proj_weight=proj_weight, gate_weight=gate_weight, out_weight=out_weight)


def layer_norm(values):
    average = lax.optimization_barrier(jnp.mean(values, axis=-1, keepdims=True))
    centered = values - average
    spread = lax.optimization_barrier(jnp.mean(centered * centered, axis=-1, keepdims=True))
    return centered * lax.rsqrt(spread + 1e-05)

def reference(pair_rep, proj_weight, gate_weight, out_weight):
    normed = layer_norm(pair_rep.astype(jnp.float32)).astype(jnp.bfloat16)
    flat_rows = normed.reshape(-1, C)
    projected = jnp.dot(flat_rows, proj_weight, preferred_element_type=jnp.float32)
    left_side = (jax.nn.sigmoid(projected[:, :CH]) * projected[:, CH:2 * CH]).astype(jnp.bfloat16)
    right_side = (jax.nn.sigmoid(projected[:, 2 * CH:3 * CH]) * projected[:, 3 * CH:]).astype(jnp.bfloat16)
    left_side = left_side.reshape(L, L, CH).astype(jnp.float32)
    right_side = right_side.reshape(L, L, CH).astype(jnp.float32)
    combined = jnp.einsum('ikc,jkc->ijc', left_side, right_side)
    tri_normed = layer_norm(combined).astype(jnp.bfloat16).reshape(-1, CH)
    gating = jax.nn.sigmoid(jnp.dot(flat_rows, gate_weight, preferred_element_type=jnp.float32))
    update = jnp.dot(tri_normed, out_weight, preferred_element_type=jnp.float32) * gating
    return update.astype(jnp.bfloat16).reshape(L, L, C)
```

```python
import functools

import jax
import jax.numpy as jnp
from jax import lax
from jax.experimental import pallas as pl
from jax.experimental.pallas import tpu as pltpu
from jax.sharding import PartitionSpec as P

F32, BF16 = jnp.float32, jnp.bfloat16
PLACED = P(("groups", "row"), "col", None)
VMEM_BUDGET = 24 * 2**20


def layer_norm(values):
    average = jnp.mean(values, axis=-1, keepdims=True)
    centered = values - average
    spread = jnp.mean(centered * centered, axis=-1, keepdims=True)
    return centered * lax.rsqrt(spread + 1e-05)


def sigmoid(values):
    return 0.5 * jnp.tanh(0.5 * values) + 0.5


def normalised(x_ref):
    x = x_ref[...].reshape(-1, x_ref.shape[-1]).astype(F32)
    return layer_norm(x).astype(BF16)


def side(normed, weight):
    both = jnp.dot(normed, weight, preferred_element_type=F32)
    hidden = both.shape[-1] // 2
    return (sigmoid(both[:, :hidden]) * both[:, hidden:]).astype(BF16).astype(F32)


def in_vmem(*arrays):
    return [pltpu.with_memory_space_constraint(a, pltpu.VMEM) for a in arrays]


def own_kernel(half, x_ref, w_ref, left_ref, right_ref):
    rows = x_ref.shape[0] * x_ref.shape[1]
    hidden = left_ref.shape[-1]
    normed = normalised(x_ref)
    left_ref[pl.ds(0, rows), :] = side(normed, w_ref[:, : 2 * hidden])
    place = lax.rem(lax.axis_index("row"), half)
    right_ref[pl.ds(pl.multiple_of(place * rows, 8), rows), :] = side(normed, w_ref[:, 2 * hidden :])


def early_kernel(half, steps, *refs):
    x_refs, (far_ref, w_ref, _, _, left_ref, right_ref) = refs[: len(steps)], refs[len(steps) :]
    rows = far_ref.shape[0] * far_ref.shape[1]
    hidden = left_ref.shape[-1]
    place = lax.rem(lax.axis_index("row"), half)
    left_ref[pl.ds(rows, rows), :] = side(normalised(far_ref), w_ref[:, : 2 * hidden])
    for step, x_ref in zip(steps, x_refs, strict=True):
        start = pl.multiple_of((place ^ step) * rows, 8)
        right_ref[pl.ds(start, rows), :] = side(normalised(x_ref), w_ref[:, 2 * hidden :])


def products(left_ref, right_ref, out_ref, strips, depth, group):
    count = out_ref.shape[0]
    for first in range(0, count, group):
        rows = range(first, min(first + group, count))

        def body(k, sums):
            rights = [right_ref[pl.ds(s * depth + k, 8, stride=depth), :] for s in strips]
            added = []
            for n, i in enumerate(rows):
                left = left_ref[pl.ds(i * depth + k, 1), :]
                added.append(tuple(a + left * r for a, r in zip(sums[n], rights, strict=True)))
            return tuple(added)

        zero = jnp.zeros((8, left_ref.shape[-1]), F32)
        sums = lax.fori_loop(0, depth, body, tuple(tuple(zero for _ in strips) for _ in rows), unroll=4)
        for n, i in enumerate(rows):
            for s, total in zip(strips, sums[n], strict=True):
                out_ref[i, pl.ds(s, 8), :] = total


def gate_kernel(half, x_ref, other_ref, g_ref, out_ref):
    ours = lax.axis_index("row") // half == lax.axis_index("col")
    x = jnp.where(ours, x_ref[...].astype(F32), other_ref[...].astype(F32))
    normed = layer_norm(x.reshape(-1, x.shape[-1])).astype(BF16)
    out_ref[...] = sigmoid(jnp.dot(normed, g_ref[...], preferred_element_type=F32))


def late_kernel(half, step, depth, x_ref, w_ref, left_ref, _, right_ref, keep_ref, give_ref):
    rows = x_ref.shape[0] * x_ref.shape[1]
    count, width = x_ref.shape[0], keep_ref.shape[1]
    hidden = left_ref.shape[-1]
    place = lax.rem(lax.axis_index("row"), half)
    ours = lax.axis_index("row") // half == lax.axis_index("col")
    start = pl.multiple_of((place ^ step) * rows, 8)
    right_ref[pl.ds(start, rows), :] = side(normalised(x_ref), w_ref[:, 2 * hidden :])
    strips = list(range(0, width, 8))

    def mine(offset):
        return left_ref.at[pl.ds(pl.multiple_of(offset * rows, 8), rows)]

    kept = jnp.where(ours, 0, 1)
    products(mine(1 - kept), right_ref, give_ref, strips, depth, 5)
    products(mine(kept), right_ref, keep_ref, strips, depth, 5)


def finish_kernel(keep_ref, got_ref, gating_ref, o_ref, out_ref):
    combined = keep_ref[...] + got_ref[...]
    tri = layer_norm(combined.reshape(-1, combined.shape[-1])).astype(BF16)
    update = jnp.dot(tri, o_ref[...], preferred_element_type=F32) * gating_ref[...]
    out_ref[...] = update.astype(BF16).reshape(out_ref.shape)


def choose_kernel(half, mine_ref, got_ref, out_ref):
    ours = lax.axis_index("row") // half == lax.axis_index("col")

    @pl.when(ours)
    def _():
        out_ref[...] = mine_ref[...]

    @pl.when(jnp.logical_not(ours))
    def _():
        out_ref[...] = got_ref[...]


def fast_plan(mesh, x, proj_weight, gate_weight, out_weight):
    rows_here, depth, _ = x.shape
    hidden = out_weight.shape[0]
    rows, half = mesh.shape["row"], mesh.shape["row"] // 2
    wide = half * rows_here
    positions = rows_here * depth
    call = functools.partial(pl.pallas_call, compiler_params=pltpu.CompilerParams(vmem_limit_bytes=40 * 2**20))

    def from_step(step):
        return lax.ppermute(x, "row", [(i, i ^ step) for i in range(rows)])

    far = from_step(half)
    steps = sorted(range(1, half), reverse=True)
    *early, last = [2, 1, 3] if half == 4 else steps
    blocks = {step: from_step(step) for step in steps}
    swap = [(0, 1), (1, 0)]
    far_other = lax.ppermute(far, "col", swap)
    x_v, w_v, g_v, o_v = in_vmem(x, proj_weight, gate_weight, out_weight)
    lefts, rights = pltpu.VMEM((2 * positions, hidden), F32), pltpu.VMEM((half * positions, hidden), F32)
    left, right = call(functools.partial(own_kernel, half), out_shape=(lefts, rights))(x_v, w_v)
    taken = in_vmem(*[blocks[s] for s in early], far)
    left, right = call(
        functools.partial(early_kernel, half, tuple(early)),
        out_shape=(lefts, rights),
        input_output_aliases={len(taken) + 1: 0, len(taken) + 2: 1},
    )(*taken, w_v, *in_vmem(left, right))
    gating = call(functools.partial(gate_kernel, half), out_shape=pltpu.VMEM((positions, hidden), F32))(
        x_v, *in_vmem(far_other), g_v
    )
    part = pltpu.VMEM((rows_here, wide, hidden), F32)
    _, keep, give = call(
        functools.partial(late_kernel, half, last, depth),
        out_shape=(rights, part, part),
        input_output_aliases={3: 0},
    )(*in_vmem(blocks[last]), w_v, *in_vmem(left, right))
    got = lax.ppermute(give, "col", swap)
    update = call(finish_kernel, out_shape=pltpu.VMEM(x.shape, BF16))(*in_vmem(keep, got, gating), o_v)
    pairs = [
        (2 * r + 1 - r // half, 2 * (r ^ half) + r // half)
        for r in range(rows)
    ]
    arrived = lax.ppermute(update, ("row", "col"), pairs)
    return call(
        functools.partial(choose_kernel, half),
        in_specs=[pl.BlockSpec(memory_space=pltpu.VMEM)] * 2,
        out_specs=pl.BlockSpec(memory_space=pltpu.VMEM),
        out_shape=jax.ShapeDtypeStruct(x.shape, BF16),
    )(*in_vmem(update, arrived))


def gather_plan(pair_rep, proj_weight, gate_weight, out_weight):
    rows_here, cols_here, channels = pair_rep.shape
    hidden = out_weight.shape[0]
    normed = layer_norm(pair_rep.astype(F32)).astype(BF16)
    flat_rows = normed.reshape(-1, channels)
    projected = jnp.dot(flat_rows, proj_weight, preferred_element_type=F32)
    left, right = (
        (jax.nn.sigmoid(projected[:, at : at + hidden]) * projected[:, at + hidden : at + 2 * hidden])
        .astype(BF16)
        .reshape(rows_here, cols_here, hidden)
        for at in (0, 2 * hidden)
    )
    gating = jax.nn.sigmoid(jnp.dot(flat_rows, gate_weight, preferred_element_type=F32))
    left_full = lax.all_gather(left, "col", axis=1, tiled=True)
    right_all = lax.all_gather(lax.all_gather(right, "col", axis=1, tiled=True), "row", axis=0, tiled=True)
    mine = lax.dynamic_slice_in_dim(right_all, lax.axis_index("col") * cols_here, cols_here, 0)
    combined = jnp.einsum("ikc,jkc->ijc", left_full, mine, preferred_element_type=F32)
    tri_normed = layer_norm(combined).astype(BF16).reshape(-1, hidden)
    update = jnp.dot(tri_normed, out_weight, preferred_element_type=F32) * gating
    return update.astype(BF16).reshape(rows_here, cols_here, channels)


def solution(mesh):
    def per_device(pair_rep, proj_weight, gate_weight, out_weight):
        rows_here, cols_here, channels = pair_rep.shape
        hidden = out_weight.shape[0]
        rows, cols = mesh.shape["row"], mesh.shape["col"]
        half = rows // 2
        held = 4 * hidden * (half + 3) * rows_here * cols_here + 12 * hidden * half * rows_here**2
        fits = held + 2 * half * pair_rep.size <= VMEM_BUDGET and channels == hidden
        even = cols == 2 and rows >= 4 and rows & (rows - 1) == 0 and half * rows_here == cols_here
        tiled = rows_here * cols_here % 16 == 0 and cols_here % 8 == 0 and channels % 128 == 0
        if fits and even and tiled:
            return fast_plan(mesh, pair_rep, proj_weight, gate_weight, out_weight)
        return gather_plan(pair_rep, proj_weight, gate_weight, out_weight)

    return jax.shard_map(
        per_device,
        mesh=mesh,
        in_specs=(PLACED, P(), P(), P()),
        out_specs=PLACED,
        check_vma=False,
    )
```

```python
import functools

import jax
import jax.numpy as jnp
from jax import lax
from jax.experimental import pallas as pl
from jax.experimental.pallas import tpu as pltpu
from jax.sharding import PartitionSpec as P

F32, BF16 = jnp.float32, jnp.bfloat16
PLACED = P(("groups", "row"), "col", None)
VMEM_BUDGET = 24 * 2**20


def layer_norm(values):
    average = jnp.mean(values, axis=-1, keepdims=True)
    centered = values - average
    spread = jnp.mean(centered * centered, axis=-1, keepdims=True)
    return centered * lax.rsqrt(spread + 1e-05)


def sigmoid(values):
    return 0.5 * jnp.tanh(0.5 * values) + 0.5


def normalised(x_ref):
    x = x_ref[...].reshape(-1, x_ref.shape[-1]).astype(F32)
    return layer_norm(x).astype(BF16)


def side(normed, weight):
    both = jnp.dot(normed, weight, preferred_element_type=F32)
    hidden = both.shape[-1] // 2
    return (sigmoid(both[:, :hidden]) * both[:, hidden:]).astype(BF16).astype(F32)


def in_vmem(*arrays):
    return [pltpu.with_memory_space_constraint(a, pltpu.VMEM) for a in arrays]


def place_of(half):
    row = lax.axis_index("row")
    return lax.rem(row, half), lax.div(row, half) == lax.axis_index("col")


def put_right(half, step, x_ref, w_ref, right_ref):
    rows, hidden = x_ref.shape[0] * x_ref.shape[1], right_ref.shape[-1]
    start = pl.multiple_of((place_of(half)[0] ^ step) * rows, 8)
    right_ref[pl.ds(start, rows), :] = side(normalised(x_ref), w_ref[:, 2 * hidden :])


def own_kernel(half, x_ref, w_ref, g_ref, o_ref, left_ref, right_ref, gate_ref, w_out, g_out, o_out, x_in, sems):
    pairs = ((x_ref, x_in), (w_ref, w_out), (g_ref, g_out), (o_ref, o_out))
    copies = [pltpu.make_async_copy(a, b, sems.at[n]) for n, (a, b) in enumerate(pairs)]
    for copy in copies:
        copy.start()
    for copy in copies:
        copy.wait()
    rows, hidden = gate_ref.shape
    normed = normalised(x_in)
    left_ref[pl.ds(0, rows), :] = side(normed, w_out[:, : 2 * hidden])
    start = pl.multiple_of(place_of(half)[0] * rows, 8)
    right_ref[pl.ds(start, rows), :] = side(normed, w_out[:, 2 * hidden :])
    gate_ref[...] = sigmoid(jnp.dot(normed, g_out[...], preferred_element_type=F32))


def products(left_ref, base, right_ref, strips, depth, out_ref, group):
    count = out_ref.shape[0]
    for first in range(0, count, group):
        rows = range(first, min(first + group, count))

        def body(k, sums):
            rights = [right_ref[pl.ds(s * depth + k, 8, stride=depth), :] for s in strips]
            added = []
            for n, i in enumerate(rows):
                left = left_ref[pl.ds(base + i * depth + k, 1), :]
                added.append(tuple(a + left * r for a, r in zip(sums[n], rights, strict=True)))
            return tuple(added)

        zero = jnp.zeros((8, left_ref.shape[-1]), F32)
        sums = lax.fori_loop(0, depth, body, tuple(tuple(zero for _ in strips) for _ in rows), unroll=4)
        for n, i in enumerate(rows):
            for s, total in zip(strips, sums[n], strict=True):
                out_ref[i, pl.ds(s, 8), :] = total


def strips_of(half, step, rows_here):
    bounds = [(p * rows_here // 8, -(-(p + 1) * rows_here // 8)) for p in range(half)]
    count, total = max(b - a for a, b in bounds), half * rows_here // 8
    first = jnp.minimum(lax.div((place_of(half)[0] ^ step) * rows_here, 8), total - count)
    early = [jnp.where(n < first, n, n + count) for n in range(total - count)]
    late = [first + n for n in range(count)]
    return [[pl.multiple_of(s * 8, 8) for s in strips] for strips in (early, late)]


def near_kernel(half, steps, last, depth, *refs):
    x_refs, (w_ref, left_ref, _, right_ref, tile_ref) = refs[: len(steps)], refs[len(steps) :]
    for step, x_ref in zip(steps, x_refs, strict=True):
        put_right(half, step, x_ref, w_ref, right_ref)
    early, _ = strips_of(half, last, tile_ref.shape[0])
    for n in range(0, len(early), 3):
        products(left_ref, 0, right_ref, early[n : n + 3], depth, tile_ref, 10)


def far_kernel(half, last, depth, far_ref, w_ref, right_ref, _, left_ref, tile_ref):
    rows, hidden = left_ref.shape[0] // 2, left_ref.shape[-1]
    left_ref[pl.ds(rows, rows), :] = side(normalised(far_ref), w_ref[:, : 2 * hidden])
    early, _ = strips_of(half, last, tile_ref.shape[0])
    for n in range(0, len(early), 3):
        products(left_ref, rows, right_ref, early[n : n + 3], depth, tile_ref, 10)


def late_kernel(half, step, depth, x_ref, w_ref, left_ref, tile_ref, other_ref, _, right_ref, keep_ref, give_ref):
    put_right(half, step, x_ref, w_ref, right_ref)
    ours = place_of(half)[1]
    keep_ref[...] = jnp.where(ours, tile_ref[...], other_ref[...])
    give_ref[...] = jnp.where(ours, other_ref[...], tile_ref[...])
    rows = left_ref.shape[0] // 2
    _, late = strips_of(half, step, keep_ref.shape[0])
    for ref, base in ((give_ref, jnp.where(ours, rows, 0)), (keep_ref, jnp.where(ours, 0, rows))):
        for n in range(0, len(late), 2):
            products(left_ref, pl.multiple_of(base, 8), right_ref, late[n : n + 2], depth, ref, 10)


def norm_kernel(keep_ref, got_ref, tri_ref):
    tri_ref[...] = layer_norm(keep_ref[...] + got_ref[...]).astype(BF16)


def finish_kernel(half, tri_ref, got_ref, gate_ref, o_ref, out_ref):
    tri = jnp.where(place_of(half)[1], tri_ref[...].astype(F32), got_ref[...].astype(F32)).astype(BF16)
    update = jnp.dot(tri.reshape(gate_ref.shape), o_ref[...], preferred_element_type=F32)
    out_ref[...] = (update * gate_ref[...]).astype(BF16).reshape(out_ref.shape)


def fast_plan(mesh, x, proj_weight, gate_weight, out_weight):
    rows_here, depth, _ = x.shape
    hidden = out_weight.shape[0]
    rows, half = mesh.shape["row"], mesh.shape["row"] // 2
    positions = rows_here * depth
    call = functools.partial(pl.pallas_call, compiler_params=pltpu.CompilerParams(vmem_limit_bytes=40 * 2**20))

    def from_step(step):
        return lax.ppermute(x, "row", [(i, i ^ step) for i in range(rows)])

    far = from_step(half)
    steps = sorted(range(1, half), reverse=True)
    *early, last = [3, 1, 2] if half == 4 else steps
    blocks = {step: from_step(step) for step in [*early, last]}
    lefts, rights = pltpu.VMEM((2 * positions, hidden), F32), pltpu.VMEM((half * positions, hidden), F32)
    part = pltpu.VMEM((rows_here, half * rows_here, hidden), F32)
    brought = (x, proj_weight, gate_weight, out_weight)
    left, right, gate, w_v, _, o_v = in_vmem(
        *call(
            functools.partial(own_kernel, half),
            in_specs=[pl.BlockSpec(memory_space=pltpu.HBM)] * 4,
            out_shape=(lefts, rights, pltpu.VMEM((positions, hidden), F32), *[pltpu.VMEM(a.shape, a.dtype) for a in brought[1:]]),
            scratch_shapes=[pltpu.VMEM(x.shape, x.dtype), pltpu.SemaphoreType.DMA((4,))],
        )(*[pltpu.with_memory_space_constraint(a, pltpu.HBM) for a in brought])
    )
    right, tile = in_vmem(
        *call(
            functools.partial(near_kernel, half, tuple(early), last, depth),
            out_shape=(rights, part),
            input_output_aliases={len(early) + 2: 0},
        )(*in_vmem(*[blocks[s] for s in early]), w_v, left, right)
    )
    left, far_tile = in_vmem(
        *call(
            functools.partial(far_kernel, half, last, depth),
            out_shape=(lefts, part),
            input_output_aliases={3: 0},
        )(*in_vmem(far), w_v, right, left)
    )
    _, keep, give = call(
        functools.partial(late_kernel, half, last, depth),
        out_shape=(rights, part, part),
        input_output_aliases={5: 0},
    )(*in_vmem(blocks[last]), w_v, left, tile, far_tile, right)
    got = lax.ppermute(give, "col", [(0, 1), (1, 0)])
    tri = call(norm_kernel, out_shape=pltpu.VMEM(x.shape, BF16))(*in_vmem(keep, got))
    pairs = [(2 * r + 1 - r // half, 2 * (r ^ half) + r // half) for r in range(rows)]
    pairs += [(2 * r + r // half, 2 * (r ^ 1) + r // half) for r in range(rows)]
    arrived = lax.ppermute(tri, ("row", "col"), pairs)
    return call(
        functools.partial(finish_kernel, half),
        in_specs=[pl.BlockSpec(memory_space=pltpu.VMEM)] * 4,
        out_specs=pl.BlockSpec(memory_space=pltpu.VMEM),
        out_shape=jax.ShapeDtypeStruct(x.shape, BF16),
    )(*in_vmem(tri, arrived), gate, o_v)


def gather_plan(pair_rep, proj_weight, gate_weight, out_weight):
    rows_here, cols_here, channels = pair_rep.shape
    hidden = out_weight.shape[0]
    normed = layer_norm(pair_rep.astype(F32)).astype(BF16)
    flat_rows = normed.reshape(-1, channels)
    projected = jnp.dot(flat_rows, proj_weight, preferred_element_type=F32)
    left, right = (
        (jax.nn.sigmoid(projected[:, at : at + hidden]) * projected[:, at + hidden : at + 2 * hidden])
        .astype(BF16)
        .reshape(rows_here, cols_here, hidden)
        for at in (0, 2 * hidden)
    )
    gating = jax.nn.sigmoid(jnp.dot(flat_rows, gate_weight, preferred_element_type=F32))
    left_full = lax.all_gather(left, "col", axis=1, tiled=True)
    right_all = lax.all_gather(lax.all_gather(right, "col", axis=1, tiled=True), "row", axis=0, tiled=True)
    mine = lax.dynamic_slice_in_dim(right_all, lax.axis_index("col") * cols_here, cols_here, 0)
    combined = jnp.einsum("ikc,jkc->ijc", left_full, mine, preferred_element_type=F32)
    tri_normed = layer_norm(combined).astype(BF16).reshape(-1, hidden)
    update = jnp.dot(tri_normed, out_weight, preferred_element_type=F32) * gating
    return update.astype(BF16).reshape(rows_here, cols_here, channels)


def solution(mesh):
    def per_device(pair_rep, proj_weight, gate_weight, out_weight):
        rows_here, cols_here, channels = pair_rep.shape
        hidden = out_weight.shape[0]
        rows, cols = mesh.shape["row"], mesh.shape["col"]
        half = rows // 2
        held = 4 * hidden * (half + 3) * rows_here * cols_here + 12 * hidden * half * rows_here**2
        fits = held + 2 * half * pair_rep.size <= VMEM_BUDGET and channels == hidden
        even = cols == 2 and rows >= 4 and rows & (rows - 1) == 0 and half * rows_here == cols_here
        tiled = rows_here * cols_here % 16 == 0 and cols_here % 8 == 0 and channels % 128 == 0
        if fits and even and tiled:
            return fast_plan(mesh, pair_rep, proj_weight, gate_weight, out_weight)
        return gather_plan(pair_rep, proj_weight, gate_weight, out_weight)

    return jax.shard_map(
        per_device,
        mesh=mesh,
        in_specs=(PLACED, P(), P(), P()),
        out_specs=PLACED,
        check_vma=False,
    )
```

```python
import functools
import itertools

import jax
import jax.numpy as jnp
from jax import lax
from jax.experimental import pallas as pl
from jax.experimental.pallas import tpu as pltpu
from jax.sharding import PartitionSpec as P

F32, BF16 = jnp.float32, jnp.bfloat16
PLACED = P(("groups", "row"), "col", None)
VMEM_BUDGET = 24 * 2**20


def layer_norm(values):
    average = jnp.mean(values, axis=-1, keepdims=True)
    centered = values - average
    spread = jnp.mean(centered * centered, axis=-1, keepdims=True)
    return centered * lax.rsqrt(spread + 1e-05)


def sigmoid(values):
    return 0.5 * jnp.tanh(0.5 * values) + 0.5


def normalised(x_ref):
    x = x_ref[...].reshape(-1, x_ref.shape[-1]).astype(F32)
    return layer_norm(x).astype(BF16)


def side(normed, weight):
    both = jnp.dot(normed, weight, preferred_element_type=F32)
    hidden = both.shape[-1] // 2
    return (sigmoid(both[:, :hidden]) * both[:, hidden:]).astype(BF16).astype(F32)


def in_vmem(*arrays):
    return [pltpu.with_memory_space_constraint(a, pltpu.VMEM) for a in arrays]


def place_of(half):
    row = lax.axis_index("row")
    return lax.rem(row, half), lax.div(row, half) == lax.axis_index("col")


def put_right(half, step, x_ref, w_ref, right_ref):
    rows, hidden = x_ref.shape[0] * x_ref.shape[1], right_ref.shape[-1]
    start = pl.multiple_of((place_of(half)[0] ^ step) * rows, 8)
    right_ref[pl.ds(start, rows), :] = side(normalised(x_ref), w_ref[:, 2 * hidden :])


def own_kernel(half, x_ref, w_ref, g_ref, o_ref, left_ref, right_ref, gate_ref, w_out, g_out, o_out, x_in, sems):
    pairs = ((x_ref, x_in), (w_ref, w_out), (g_ref, g_out), (o_ref, o_out))
    copies = [pltpu.make_async_copy(a, b, sems.at[n]) for n, (a, b) in enumerate(pairs)]
    for copy in copies:
        copy.start()
    for copy in copies:
        copy.wait()
    rows, hidden = gate_ref.shape
    normed = normalised(x_in)
    left_ref[pl.ds(0, rows), :] = side(normed, w_out[:, : 2 * hidden])
    start = pl.multiple_of(place_of(half)[0] * rows, 8)
    right_ref[pl.ds(start, rows), :] = side(normed, w_out[:, 2 * hidden :])
    gate_ref[...] = sigmoid(jnp.dot(normed, g_out[...], preferred_element_type=F32))


def products(left_ref, base, right_ref, strips, places, out_ref):
    count = out_ref.shape[0]
    depth = left_ref.shape[0] // (2 * count)
    for first, at in itertools.product(range(0, count, 10), range(0, len(strips), 3)):
        rows, some = range(first, min(first + 10, count)), strips[at : at + 3]

        def body(k, sums):
            rights = [right_ref[pl.ds(s * depth + k, 8, stride=depth), :] for s in some]
            added = []
            for n, i in enumerate(rows):
                left = left_ref[pl.ds(base + i * depth + k, 1), :]
                added.append(tuple(a + left * r for a, r in zip(sums[n], rights, strict=True)))
            return tuple(added)

        zero = jnp.zeros((8, left_ref.shape[-1]), F32)
        sums = lax.fori_loop(0, depth, body, tuple(tuple(zero for _ in some) for _ in rows), unroll=4)
        for n, i in enumerate(rows):
            for place, total in zip(places[at : at + 3], sums[n], strict=True):
                out_ref[i, pl.ds(place, 8), :] = total


def strips_of(half, rows_here):
    part = half // 2 * rows_here
    total = half * rows_here // 8
    count = min(part // 8, total - -(-part // 8))
    second = lax.div(place_of(half)[0], half // 2)
    early = [second * (total - count) + n for n in range(count)]
    late = [(1 - second) * count + n for n in range(total - count)]
    return [[pl.multiple_of(s * 8, 8) for s in strips] for strips in (early, late)]


def right_kernel(half, step, x_ref, w_ref, _, right_ref):
    put_right(half, step, x_ref, w_ref, right_ref)


def near_kernel(half, step, x_ref, w_ref, left_ref, _, right_ref, tile_ref):
    put_right(half, step, x_ref, w_ref, right_ref)
    early, _ = strips_of(half, tile_ref.shape[0])
    products(left_ref, 0, right_ref, early, range(0, tile_ref.shape[1], 8), tile_ref)


def far_kernel(half, far_ref, w_ref, right_ref, _, left_ref, tile_ref):
    rows, hidden = left_ref.shape[0] // 2, left_ref.shape[-1]
    left_ref[pl.ds(rows, rows), :] = side(normalised(far_ref), w_ref[:, : 2 * hidden])
    early, _ = strips_of(half, tile_ref.shape[0])
    products(left_ref, rows, right_ref, early, range(0, tile_ref.shape[1], 8), tile_ref)


def whole_tile(half, given, left_ref, right_ref, own_ref, far_ref, out_ref):
    own = place_of(half)[1] != given
    early, late = strips_of(half, out_ref.shape[0])
    for n, s in enumerate(early):
        here = slice(8 * n, 8 * n + 8)
        out_ref[:, pl.ds(s, 8), :] = jnp.where(own, own_ref[:, here, :], far_ref[:, here, :])
    base = pl.multiple_of(jnp.where(own, 0, left_ref.shape[0] // 2), 8)
    products(left_ref, base, right_ref, late, late, out_ref)


def late_kernel(half, step, x_ref, w_ref, left_ref, own_ref, far_ref, _, right_ref, give_ref):
    put_right(half, step, x_ref, w_ref, right_ref)
    whole_tile(half, True, left_ref, right_ref, own_ref, far_ref, give_ref)


def norm_kernel(keep_ref, got_ref, tri_ref):
    tri_ref[...] = layer_norm(keep_ref[...] + got_ref[...]).astype(BF16)


def finish_kernel(half, tri_ref, got_ref, gate_ref, o_ref, out_ref):
    tri = jnp.where(place_of(half)[1], tri_ref[...].astype(F32), got_ref[...].astype(F32)).astype(BF16)
    update = jnp.dot(tri.reshape(gate_ref.shape), o_ref[...], preferred_element_type=F32)
    out_ref[...] = (update * gate_ref[...]).astype(BF16).reshape(out_ref.shape)


def fast_plan(mesh, x, proj_weight, gate_weight, out_weight):
    rows_here, depth, _ = x.shape
    hidden = out_weight.shape[0]
    rows, half = mesh.shape["row"], mesh.shape["row"] // 2
    positions = rows_here * depth
    call = functools.partial(pl.pallas_call, compiler_params=pltpu.CompilerParams(vmem_limit_bytes=40 * 2**20))

    def from_step(step):
        return lax.ppermute(x, "row", [(i, i ^ step) for i in range(rows)])

    far = from_step(half)
    blocks = {step: from_step(step) for step in range(1, half)}
    lefts, rights = pltpu.VMEM((2 * positions, hidden), F32), pltpu.VMEM((half * positions, hidden), F32)
    brought = (x, proj_weight, gate_weight, out_weight)
    left, right, gate, w_v, _, o_v = in_vmem(
        *call(
            functools.partial(own_kernel, half),
            in_specs=[pl.BlockSpec(memory_space=pltpu.HBM)] * 4,
            out_shape=(lefts, rights, pltpu.VMEM((positions, hidden), F32), *[pltpu.VMEM(a.shape, a.dtype) for a in brought[1:]]),
            scratch_shapes=[pltpu.VMEM(x.shape, x.dtype), pltpu.SemaphoreType.DMA((4,))],
        )(*[pltpu.with_memory_space_constraint(a, pltpu.HBM) for a in brought])
    )

    def with_block(step, right):
        body = functools.partial(right_kernel, half, step)
        return call(body, out_shape=rights, input_output_aliases={2: 0})(*in_vmem(blocks[step]), w_v, *in_vmem(right))

    def with_far(left, right):
        return in_vmem(
            *call(functools.partial(far_kernel, half), out_shape=(lefts, early_part), input_output_aliases={3: 0})(
                *in_vmem(far), w_v, *in_vmem(right), left
            )
        )

    for step in range(half // 2 - 1, 1, -1):
        right = with_block(step, right)
    early_part = pltpu.VMEM((rows_here, 8 * len(strips_of(half, rows_here)[0]), hidden), F32)
    tile_part = pltpu.VMEM((rows_here, half * rows_here, hidden), F32)
    right, own_early = in_vmem(
        *call(functools.partial(near_kernel, half, 1), out_shape=(rights, early_part), input_output_aliases={3: 0})(
            *in_vmem(blocks[1]), w_v, left, *in_vmem(right)
        )
    )
    for step in range(half - 1, half // 2, -1):
        right = with_block(step, right)
    left, far_early = with_far(left, right)
    right, give = in_vmem(
        *call(
            functools.partial(late_kernel, half, half // 2), out_shape=(rights, tile_part), input_output_aliases={5: 0}
        )(*in_vmem(blocks[half // 2]), w_v, left, own_early, far_early, *in_vmem(right))
    )
    got = lax.ppermute(give, "col", [(0, 1), (1, 0)])
    keep = call(functools.partial(whole_tile, half, False), out_shape=tile_part)(left, right, own_early, far_early)
    tri = call(norm_kernel, out_shape=pltpu.VMEM(x.shape, BF16))(*in_vmem(keep, got))
    pairs = [(2 * r + 1 - r // half, 2 * (r ^ half) + r // half) for r in range(rows)]
    pairs += [(2 * r + r // half, 2 * (r ^ 1) + r // half) for r in range(rows)]
    arrived = lax.ppermute(tri, ("row", "col"), pairs)
    return call(
        functools.partial(finish_kernel, half),
        in_specs=[pl.BlockSpec(memory_space=pltpu.VMEM)] * 4,
        out_specs=pl.BlockSpec(memory_space=pltpu.VMEM),
        out_shape=jax.ShapeDtypeStruct(x.shape, BF16),
    )(*in_vmem(tri, arrived), gate, o_v)


def gather_plan(pair_rep, proj_weight, gate_weight, out_weight):
    rows_here, cols_here, channels = pair_rep.shape
    hidden = out_weight.shape[0]
    normed = layer_norm(pair_rep.astype(F32)).astype(BF16)
    flat_rows = normed.reshape(-1, channels)
    projected = jnp.dot(flat_rows, proj_weight, preferred_element_type=F32)
    left, right = (
        (jax.nn.sigmoid(projected[:, at : at + hidden]) * projected[:, at + hidden : at + 2 * hidden])
        .astype(BF16)
        .reshape(rows_here, cols_here, hidden)
        for at in (0, 2 * hidden)
    )
    gating = jax.nn.sigmoid(jnp.dot(flat_rows, gate_weight, preferred_element_type=F32))
    left_full = lax.all_gather(left, "col", axis=1, tiled=True)
    right_all = lax.all_gather(lax.all_gather(right, "col", axis=1, tiled=True), "row", axis=0, tiled=True)
    mine = lax.dynamic_slice_in_dim(right_all, lax.axis_index("col") * cols_here, cols_here, 0)
    combined = jnp.einsum("ikc,jkc->ijc", left_full, mine, preferred_element_type=F32)
    tri_normed = layer_norm(combined).astype(BF16).reshape(-1, hidden)
    update = jnp.dot(tri_normed, out_weight, preferred_element_type=F32) * gating
    return update.astype(BF16).reshape(rows_here, cols_here, channels)


def solution(mesh):
    def per_device(pair_rep, proj_weight, gate_weight, out_weight):
        rows_here, cols_here, channels = pair_rep.shape
        hidden = out_weight.shape[0]
        rows, cols = mesh.shape["row"], mesh.shape["col"]
        half = rows // 2
        held = 4 * hidden * (half + 3) * rows_here * cols_here + 12 * hidden * half * rows_here**2
        fits = held + 2 * half * pair_rep.size <= VMEM_BUDGET and channels == hidden
        even = cols == 2 and rows >= 4 and rows & (rows - 1) == 0 and half * rows_here == cols_here
        tiled = rows_here * cols_here % 16 == 0 and cols_here % 8 == 0 and channels % 128 == 0
        if fits and even and tiled:
            return fast_plan(mesh, pair_rep, proj_weight, gate_weight, out_weight)
        return gather_plan(pair_rep, proj_weight, gate_weight, out_weight)

    return jax.shard_map(
        per_device,
        mesh=mesh,
        in_specs=(PLACED, P(), P(), P()),
        out_specs=PLACED,
        check_vma=False,
    )
```

```python
import functools
import itertools

import jax
import jax.numpy as jnp
from jax import lax
from jax.experimental import pallas as pl
from jax.experimental.pallas import tpu as pltpu
from jax.sharding import PartitionSpec as P

F32, BF16 = jnp.float32, jnp.bfloat16
PLACED = P(("groups", "row"), "col", None)
VMEM_BUDGET = 24 * 2**20


def layer_norm(values):
    average = jnp.mean(values, axis=-1, keepdims=True)
    centered = values - average
    spread = jnp.mean(centered * centered, axis=-1, keepdims=True)
    return centered * lax.rsqrt(spread + 1e-05)


def sigmoid(values):
    return 0.5 * jnp.tanh(0.5 * values) + 0.5


def normalised(x_ref):
    x = x_ref[...].reshape(-1, x_ref.shape[-1]).astype(F32)
    return layer_norm(x).astype(BF16)


def side(normed, weight):
    both = jnp.dot(normed, weight, preferred_element_type=F32)
    hidden = both.shape[-1] // 2
    return (sigmoid(both[:, :hidden]) * both[:, hidden:]).astype(BF16).astype(F32)


def in_vmem(*arrays):
    return [pltpu.with_memory_space_constraint(a, pltpu.VMEM) for a in arrays]


def place_of(half):
    row = lax.axis_index("row")
    return lax.rem(row, half), lax.div(row, half) == lax.axis_index("col")


def put_right(half, step, x_ref, w_ref, right_ref):
    rows, hidden = x_ref.shape[0] * x_ref.shape[1], right_ref.shape[-1]
    start = pl.multiple_of((place_of(half)[0] ^ step) * rows, 8)
    right_ref[pl.ds(start, rows), :] = side(normalised(x_ref), w_ref[:, 2 * hidden :])


def own_kernel(half, x_ref, w_ref, g_ref, o_ref, left_ref, right_ref, gate_ref, w_out, g_out, o_out, x_in, sems):
    pairs = ((x_ref, x_in), (w_ref, w_out), (g_ref, g_out), (o_ref, o_out))
    copies = [pltpu.make_async_copy(a, b, sems.at[n]) for n, (a, b) in enumerate(pairs)]
    for copy in copies:
        copy.start()
    for copy in copies:
        copy.wait()
    rows, hidden = gate_ref.shape
    normed = normalised(x_in)
    left_ref[pl.ds(0, rows), :] = side(normed, w_out[:, : 2 * hidden])
    start = pl.multiple_of(place_of(half)[0] * rows, 8)
    right_ref[pl.ds(start, rows), :] = side(normed, w_out[:, 2 * hidden :])
    gate_ref[...] = sigmoid(jnp.dot(normed, g_out[...], preferred_element_type=F32))


def products(left_ref, base, right_ref, strips, places, out_ref):
    count = out_ref.shape[0]
    depth = left_ref.shape[0] // (2 * count)
    for first, at in itertools.product(range(0, count, 10), range(0, len(strips), 3)):
        rows, some = range(first, min(first + 10, count)), strips[at : at + 3]

        def body(k, sums):
            rights = [right_ref[pl.ds(s * depth + k, 8, stride=depth), :] for s in some]
            added = []
            for n, i in enumerate(rows):
                left = left_ref[pl.ds(base + i * depth + k, 1), :]
                added.append(tuple(a + left * r for a, r in zip(sums[n], rights, strict=True)))
            return tuple(added)

        zero = jnp.zeros((8, left_ref.shape[-1]), F32)
        sums = lax.fori_loop(0, depth, body, tuple(tuple(zero for _ in some) for _ in rows), unroll=4)
        for n, i in enumerate(rows):
            for place, total in zip(places[at : at + 3], sums[n], strict=True):
                out_ref[i, pl.ds(place, 8), :] = total


def strips_of(half, rows_here):
    part, total = half // 2, half * rows_here // 8
    count = min(part * rows_here // 8, total - -(-part * rows_here // 8))
    place = place_of(half)[0]
    second = lax.div(place, part)
    bounds = [(p * rows_here // 8, -(-(p + 1) * rows_here // 8)) for p in range(half)]
    held, others = max(b - a for a, b in bounds), total - count
    start = (1 - second) * count
    first = jnp.clip(lax.div((place ^ part) * rows_here, 8) - start, 0, others - held)
    early = [second * others + n for n in range(count)]
    middle = [start + jnp.where(n < first, n, n + held) for n in range(others - held)]
    late = [start + first + n for n in range(held)]
    return [[pl.multiple_of(s * 8, 8) for s in strips] for strips in (early, middle, late)]


def right_kernel(half, step, x_ref, w_ref, _, right_ref):
    put_right(half, step, x_ref, w_ref, right_ref)


def middle_kernel(half, step, x_ref, w_ref, left_ref, _, right_ref, own_ref):
    put_right(half, step, x_ref, w_ref, right_ref)
    _, middle, _ = strips_of(half, own_ref.shape[0])
    products(left_ref, 0, right_ref, middle, range(0, own_ref.shape[1], 8), own_ref)


def near_kernel(half, step, x_ref, w_ref, left_ref, _, right_ref, tile_ref):
    put_right(half, step, x_ref, w_ref, right_ref)
    early, _, _ = strips_of(half, tile_ref.shape[0])
    products(left_ref, 0, right_ref, early, range(0, tile_ref.shape[1], 8), tile_ref)


def far_kernel(half, far_ref, w_ref, right_ref, _, left_ref, tile_ref):
    rows, hidden = left_ref.shape[0] // 2, left_ref.shape[-1]
    left_ref[pl.ds(rows, rows), :] = side(normalised(far_ref), w_ref[:, : 2 * hidden])
    early, middle, _ = strips_of(half, tile_ref.shape[0])
    products(left_ref, rows, right_ref, early + middle, range(0, tile_ref.shape[1], 8), tile_ref)


def whole_tile(half, given, left_ref, right_ref, own_ref, middle_ref, far_ref, out_ref):
    own = place_of(half)[1] != given
    early, middle, late = strips_of(half, out_ref.shape[0])
    for strips, mine_ref, at in ((early, own_ref, 0), (middle, middle_ref, len(early))):
        for n, s in enumerate(strips):
            mine, far = mine_ref[:, 8 * n : 8 * n + 8, :], far_ref[:, 8 * (at + n) : 8 * (at + n) + 8, :]
            out_ref[:, pl.ds(s, 8), :] = jnp.where(own, mine, far)
    base = pl.multiple_of(jnp.where(own, 0, left_ref.shape[0] // 2), 8)
    products(left_ref, base, right_ref, late, late, out_ref)


def late_kernel(half, step, x_ref, w_ref, left_ref, own_ref, middle_ref, far_ref, _, right_ref, give_ref):
    put_right(half, step, x_ref, w_ref, right_ref)
    whole_tile(half, True, left_ref, right_ref, own_ref, middle_ref, far_ref, give_ref)


def norm_kernel(keep_ref, got_ref, tri_ref):
    tri_ref[...] = layer_norm(keep_ref[...] + got_ref[...]).astype(BF16)


def finish_kernel(half, tri_ref, got_ref, gate_ref, o_ref, out_ref):
    tri = jnp.where(place_of(half)[1], tri_ref[...].astype(F32), got_ref[...].astype(F32)).astype(BF16)
    update = jnp.dot(tri.reshape(gate_ref.shape), o_ref[...], preferred_element_type=F32)
    out_ref[...] = (update * gate_ref[...]).astype(BF16).reshape(out_ref.shape)


def fast_plan(mesh, x, proj_weight, gate_weight, out_weight):
    rows_here, depth, _ = x.shape
    hidden = out_weight.shape[0]
    rows, half = mesh.shape["row"], mesh.shape["row"] // 2
    positions = rows_here * depth
    call = functools.partial(pl.pallas_call, compiler_params=pltpu.CompilerParams(vmem_limit_bytes=40 * 2**20))

    def from_step(step):
        return lax.ppermute(x, "row", [(i, i ^ step) for i in range(rows)])

    far = from_step(half)
    blocks = {step: from_step(step) for step in range(1, half)}
    lefts, rights = pltpu.VMEM((2 * positions, hidden), F32), pltpu.VMEM((half * positions, hidden), F32)
    brought = (x, proj_weight, gate_weight, out_weight)
    left, right, gate, w_v, _, o_v = in_vmem(
        *call(
            functools.partial(own_kernel, half),
            in_specs=[pl.BlockSpec(memory_space=pltpu.HBM)] * 4,
            out_shape=(lefts, rights, pltpu.VMEM((positions, hidden), F32), *[pltpu.VMEM(a.shape, a.dtype) for a in brought[1:]]),
            scratch_shapes=[pltpu.VMEM(x.shape, x.dtype), pltpu.SemaphoreType.DMA((4,))],
        )(*[pltpu.with_memory_space_constraint(a, pltpu.HBM) for a in brought])
    )

    def with_block(step, right):
        body = functools.partial(right_kernel, half, step)
        return call(body, out_shape=rights, input_output_aliases={2: 0})(*in_vmem(blocks[step]), w_v, *in_vmem(right))

    for step in range(half // 2 - 1, 1, -1):
        right = with_block(step, right)
    early, middle, _ = strips_of(half, rows_here)
    early_part, middle_part, far_part = (
        pltpu.VMEM((rows_here, 8 * len(strips), hidden), F32) for strips in (early, middle, early + middle)
    )
    tile_part = pltpu.VMEM((rows_here, half * rows_here, hidden), F32)
    right, own_early = in_vmem(
        *call(functools.partial(near_kernel, half, 1), out_shape=(rights, early_part), input_output_aliases={3: 0})(
            *in_vmem(blocks[1]), w_v, left, *in_vmem(right)
        )
    )
    for step in range(half - 1, half // 2 + 1, -1):
        right = with_block(step, right)
    step = half // 2 + 1
    right, own_middle = in_vmem(
        *call(
            functools.partial(middle_kernel, half, step), out_shape=(rights, middle_part), input_output_aliases={3: 0}
        )(*in_vmem(blocks[step]), w_v, left, *in_vmem(right))
    )
    left, far_sums = in_vmem(
        *call(functools.partial(far_kernel, half), out_shape=(lefts, far_part), input_output_aliases={3: 0})(
            *in_vmem(far), w_v, right, left
        )
    )
    right, give = in_vmem(
        *call(
            functools.partial(late_kernel, half, half // 2), out_shape=(rights, tile_part), input_output_aliases={6: 0}
        )(*in_vmem(blocks[half // 2]), w_v, left, own_early, own_middle, far_sums, *in_vmem(right))
    )
    got = lax.ppermute(give, "col", [(0, 1), (1, 0)])
    keep = call(functools.partial(whole_tile, half, False), out_shape=tile_part)(
        left, right, own_early, own_middle, far_sums
    )
    tri = call(norm_kernel, out_shape=pltpu.VMEM(x.shape, BF16))(*in_vmem(keep, got))
    pairs = [(2 * r + 1 - r // half, 2 * (r ^ half) + r // half) for r in range(rows)]
    pairs += [(2 * r + r // half, 2 * (r ^ 1) + r // half) for r in range(rows)]
    arrived = lax.ppermute(tri, ("row", "col"), pairs)
    return call(
        functools.partial(finish_kernel, half),
        in_specs=[pl.BlockSpec(memory_space=pltpu.VMEM)] * 4,
        out_specs=pl.BlockSpec(memory_space=pltpu.VMEM),
        out_shape=jax.ShapeDtypeStruct(x.shape, BF16),
    )(*in_vmem(tri, arrived), gate, o_v)


def gather_plan(pair_rep, proj_weight, gate_weight, out_weight):
    rows_here, cols_here, channels = pair_rep.shape
    hidden = out_weight.shape[0]
    normed = layer_norm(pair_rep.astype(F32)).astype(BF16)
    flat_rows = normed.reshape(-1, channels)
    projected = jnp.dot(flat_rows, proj_weight, preferred_element_type=F32)
    left, right = (
        (jax.nn.sigmoid(projected[:, at : at + hidden]) * projected[:, at + hidden : at + 2 * hidden])
        .astype(BF16)
        .reshape(rows_here, cols_here, hidden)
        for at in (0, 2 * hidden)
    )
    gating = jax.nn.sigmoid(jnp.dot(flat_rows, gate_weight, preferred_element_type=F32))
    left_full = lax.all_gather(left, "col", axis=1, tiled=True)
    right_all = lax.all_gather(lax.all_gather(right, "col", axis=1, tiled=True), "row", axis=0, tiled=True)
    mine = lax.dynamic_slice_in_dim(right_all, lax.axis_index("col") * cols_here, cols_here, 0)
    combined = jnp.einsum("ikc,jkc->ijc", left_full, mine, preferred_element_type=F32)
    tri_normed = layer_norm(combined).astype(BF16).reshape(-1, hidden)
    update = jnp.dot(tri_normed, out_weight, preferred_element_type=F32) * gating
    return update.astype(BF16).reshape(rows_here, cols_here, channels)


def solution(mesh):
    def per_device(pair_rep, proj_weight, gate_weight, out_weight):
        rows_here, cols_here, channels = pair_rep.shape
        hidden = out_weight.shape[0]
        rows, cols = mesh.shape["row"], mesh.shape["col"]
        half = rows // 2
        held = 4 * hidden * (half + 3) * rows_here * cols_here + 12 * hidden * half * rows_here**2
        fits = held + 2 * half * pair_rep.size <= VMEM_BUDGET and channels == hidden
        even = cols == 2 and rows >= 4 and rows & (rows - 1) == 0 and half * rows_here == cols_here
        tiled = rows_here * cols_here % 16 == 0 and cols_here % 8 == 0 and channels % 128 == 0
        if fits and even and tiled:
            return fast_plan(mesh, pair_rep, proj_weight, gate_weight, out_weight)
        return gather_plan(pair_rep, proj_weight, gate_weight, out_weight)

    return jax.shard_map(
        per_device,
        mesh=mesh,
        in_specs=(PLACED, P(), P(), P()),
        out_specs=PLACED,
        check_vma=False,
    )
```

```python
import functools
import itertools

import jax
import jax.numpy as jnp
from jax import lax
from jax.experimental import pallas as pl
from jax.experimental.pallas import tpu as pltpu
from jax.sharding import PartitionSpec as P

F32, BF16 = jnp.float32, jnp.bfloat16
PLACED = P(("groups", "row"), "col", None)
VMEM_BUDGET = 24 * 2**20


def layer_norm(values):
    average = jnp.mean(values, axis=-1, keepdims=True)
    centered = values - average
    spread = jnp.mean(centered * centered, axis=-1, keepdims=True)
    return centered * lax.rsqrt(spread + 1e-05)


def sigmoid(values):
    return 0.5 * jnp.tanh(0.5 * values) + 0.5


def normalised(x_ref):
    x = x_ref[...].reshape(-1, x_ref.shape[-1]).astype(F32)
    return layer_norm(x).astype(BF16)


def side(normed, weight):
    both = jnp.dot(normed, weight, preferred_element_type=F32)
    hidden = both.shape[-1] // 2
    return (sigmoid(both[:, :hidden]) * both[:, hidden:]).astype(BF16).astype(F32)


def in_vmem(*arrays):
    return [pltpu.with_memory_space_constraint(a, pltpu.VMEM) for a in arrays]


def place_of(half):
    row = lax.axis_index("row")
    return lax.rem(row, half), lax.div(row, half) == lax.axis_index("col")


def put_right(half, step, x_ref, w_ref, right_ref):
    rows, hidden = x_ref.shape[0] * x_ref.shape[1], right_ref.shape[-1]
    start = pl.multiple_of((place_of(half)[0] ^ step) * rows, 8)
    right_ref[pl.ds(start, rows), :] = side(normalised(x_ref), w_ref[:, 2 * hidden :])


def own_kernel(half, x_ref, w_ref, g_ref, o_ref, left_ref, right_ref, gate_ref, w_out, g_out, o_out, x_in, sems):
    pairs = ((x_ref, x_in), (w_ref, w_out), (g_ref, g_out), (o_ref, o_out))
    copies = [pltpu.make_async_copy(a, b, sems.at[n]) for n, (a, b) in enumerate(pairs)]
    for copy in copies:
        copy.start()
    for copy in copies:
        copy.wait()
    rows, hidden = gate_ref.shape
    normed = normalised(x_in)
    left_ref[pl.ds(0, rows), :] = side(normed, w_out[:, : 2 * hidden])
    start = pl.multiple_of(place_of(half)[0] * rows, 8)
    right_ref[pl.ds(start, rows), :] = side(normed, w_out[:, 2 * hidden :])
    gate_ref[...] = sigmoid(jnp.dot(normed, g_out[...], preferred_element_type=F32))


def products(left_ref, base, right_ref, strips, places, out_ref):
    count = out_ref.shape[0]
    depth = left_ref.shape[0] // (2 * count)
    for first, at in itertools.product(range(0, count, 10), range(0, len(strips), 3)):
        rows, some = range(first, min(first + 10, count)), strips[at : at + 3]

        def body(k, sums):
            rights = [right_ref[pl.ds(s * depth + k, 8, stride=depth), :] for s in some]
            added = []
            for n, i in enumerate(rows):
                left = left_ref[pl.ds(base + i * depth + k, 1), :]
                added.append(tuple(a + left * r for a, r in zip(sums[n], rights, strict=True)))
            return tuple(added)

        zero = jnp.zeros((8, left_ref.shape[-1]), F32)
        sums = lax.fori_loop(0, depth, body, tuple(tuple(zero for _ in some) for _ in rows), unroll=4)
        for n, i in enumerate(rows):
            for place, total in zip(places[at : at + 3], sums[n], strict=True):
                out_ref[i, pl.ds(place, 8), :] = total


def strips_of(half, rows_here):
    part, total = half // 2, half * rows_here // 8
    count = min(part * rows_here // 8, total - -(-part * rows_here // 8))
    place = place_of(half)[0]
    second = lax.div(place, part)
    bounds = [(p * rows_here // 8, -(-(p + 1) * rows_here // 8)) for p in range(half)]
    held, others = max(b - a for a, b in bounds), total - count
    start = (1 - second) * count
    first = jnp.clip(lax.div((place ^ part) * rows_here, 8) - start, 0, others - held)
    early = [second * others + n for n in range(count)]
    middle = [start + jnp.where(n < first, n, n + held) for n in range(others - held)]
    late = [start + first + n for n in range(held)]
    return [[pl.multiple_of(s * 8, 8) for s in strips] for strips in (early, middle, late)]


def right_kernel(half, step, x_ref, w_ref, _, right_ref):
    put_right(half, step, x_ref, w_ref, right_ref)


def middle_kernel(half, step, x_ref, w_ref, left_ref, _, right_ref, own_ref):
    put_right(half, step, x_ref, w_ref, right_ref)
    _, middle, _ = strips_of(half, own_ref.shape[0])

    @pl.when(jnp.logical_not(place_of(half)[1]))
    def _():
        products(left_ref, 0, right_ref, middle, range(0, own_ref.shape[1], 8), own_ref)


def near_kernel(half, step, x_ref, w_ref, left_ref, _, right_ref, tile_ref):
    put_right(half, step, x_ref, w_ref, right_ref)
    early, _, _ = strips_of(half, tile_ref.shape[0])
    products(left_ref, 0, right_ref, early, range(0, tile_ref.shape[1], 8), tile_ref)


def far_kernel(half, far_ref, w_ref, right_ref, _, left_ref, tile_ref):
    rows, hidden = left_ref.shape[0] // 2, left_ref.shape[-1]
    left_ref[pl.ds(rows, rows), :] = side(normalised(far_ref), w_ref[:, : 2 * hidden])
    early, middle, _ = strips_of(half, tile_ref.shape[0])

    @pl.when(place_of(half)[1])
    def _():
        products(left_ref, rows, right_ref, early + middle, range(0, tile_ref.shape[1], 8), tile_ref)


def late_kernel(half, step, x_ref, w_ref, left_ref, own_ref, middle_ref, far_ref, _, right_ref, give_ref):
    put_right(half, step, x_ref, w_ref, right_ref)
    ours = place_of(half)[1]
    early, middle, late = strips_of(half, give_ref.shape[0])
    for strips, mine_ref, at in ((early, own_ref, 0), (middle, middle_ref, len(early))):
        for n, s in enumerate(strips):
            mine, far = mine_ref[:, 8 * n : 8 * n + 8, :], far_ref[:, 8 * (at + n) : 8 * (at + n) + 8, :]
            give_ref[:, pl.ds(s, 8), :] = jnp.where(ours, far, mine)
    base = pl.multiple_of(jnp.where(ours, left_ref.shape[0] // 2, 0), 8)
    products(left_ref, base, right_ref, late, late, give_ref)


def keep_kernel(half, left_ref, right_ref, own_ref, keep_ref):
    ours = place_of(half)[1]
    early, middle, late = strips_of(half, keep_ref.shape[0])

    @pl.when(ours)
    def _():
        for n, s in enumerate(early):
            keep_ref[:, pl.ds(s, 8), :] = own_ref[:, 8 * n : 8 * n + 8, :]
        products(left_ref, 0, right_ref, middle + late, middle + late, keep_ref)

    @pl.when(jnp.logical_not(ours))
    def _():
        strips = early + middle + late
        products(left_ref, left_ref.shape[0] // 2, right_ref, strips, strips, keep_ref)


def norm_kernel(keep_ref, got_ref, tri_ref):
    tri_ref[...] = layer_norm(keep_ref[...] + got_ref[...]).astype(BF16)


def finish_kernel(half, kept, tri_ref, gate_ref, o_ref, *refs):
    out_ref, done_ref, sem = refs[-3:]

    @pl.when(place_of(half)[1] == kept)
    def _():
        update = jnp.dot(tri_ref[...].reshape(gate_ref.shape), o_ref[...], preferred_element_type=F32)
        done_ref[...] = (update * gate_ref[...]).astype(BF16).reshape(done_ref.shape)
        copy = pltpu.make_async_copy(done_ref, out_ref, sem)
        copy.start()
        copy.wait()


def fast_plan(mesh, x, proj_weight, gate_weight, out_weight):
    rows_here, depth, _ = x.shape
    hidden = out_weight.shape[0]
    rows, half = mesh.shape["row"], mesh.shape["row"] // 2
    positions = rows_here * depth
    call = functools.partial(pl.pallas_call, compiler_params=pltpu.CompilerParams(vmem_limit_bytes=40 * 2**20))

    def from_step(step):
        return lax.ppermute(x, "row", [(i, i ^ step) for i in range(rows)])

    far = from_step(half)
    blocks = {step: from_step(step) for step in range(1, half)}
    lefts, rights = pltpu.VMEM((2 * positions, hidden), F32), pltpu.VMEM((half * positions, hidden), F32)
    brought = (x, proj_weight, gate_weight, out_weight)
    left, right, gate, w_v, _, o_v = in_vmem(
        *call(
            functools.partial(own_kernel, half),
            in_specs=[pl.BlockSpec(memory_space=pltpu.HBM)] * 4,
            out_shape=(lefts, rights, pltpu.VMEM((positions, hidden), F32), *[pltpu.VMEM(a.shape, a.dtype) for a in brought[1:]]),
            scratch_shapes=[pltpu.VMEM(x.shape, x.dtype), pltpu.SemaphoreType.DMA((4,))],
        )(*[pltpu.with_memory_space_constraint(a, pltpu.HBM) for a in brought])
    )

    def with_block(step, right):
        body = functools.partial(right_kernel, half, step)
        return call(body, out_shape=rights, input_output_aliases={2: 0})(*in_vmem(blocks[step]), w_v, *in_vmem(right))

    for step in range(half // 2 - 1, 1, -1):
        right = with_block(step, right)
    early, middle, _ = strips_of(half, rows_here)
    early_part, middle_part, far_part = (
        pltpu.VMEM((rows_here, 8 * len(strips), hidden), F32) for strips in (early, middle, early + middle)
    )
    tile_part = pltpu.VMEM((rows_here, half * rows_here, hidden), F32)
    right, own_early = in_vmem(
        *call(functools.partial(near_kernel, half, 1), out_shape=(rights, early_part), input_output_aliases={3: 0})(
            *in_vmem(blocks[1]), w_v, left, *in_vmem(right)
        )
    )
    for step in range(half - 1, half // 2 + 1, -1):
        right = with_block(step, right)
    step = half // 2 + 1
    right, own_middle = in_vmem(
        *call(
            functools.partial(middle_kernel, half, step), out_shape=(rights, middle_part), input_output_aliases={3: 0}
        )(*in_vmem(blocks[step]), w_v, left, *in_vmem(right))
    )
    left, far_sums = in_vmem(
        *call(functools.partial(far_kernel, half), out_shape=(lefts, far_part), input_output_aliases={3: 0})(
            *in_vmem(far), w_v, right, left
        )
    )
    right, give = in_vmem(
        *call(
            functools.partial(late_kernel, half, half // 2), out_shape=(rights, tile_part), input_output_aliases={6: 0}
        )(*in_vmem(blocks[half // 2]), w_v, left, own_early, own_middle, far_sums, *in_vmem(right))
    )
    got = lax.ppermute(give, "col", [(0, 1), (1, 0)])
    keep = call(functools.partial(keep_kernel, half), out_shape=tile_part)(left, right, own_early)
    (tri,) = in_vmem(call(norm_kernel, out_shape=pltpu.VMEM(x.shape, BF16))(*in_vmem(keep, got)))
    pairs = [(2 * r + 1 - r // half, 2 * (r ^ half) + r // half) for r in range(rows)]
    pairs += [(2 * r + r // half, 2 * (r ^ 1) + r // half) for r in range(rows)]
    arrived = lax.ppermute(tri, ("row", "col"), pairs)
    in_place = pl.BlockSpec(memory_space=pltpu.VMEM)
    in_hbm = pl.BlockSpec(memory_space=pltpu.HBM)
    scratch = [pltpu.VMEM(x.shape, BF16), pltpu.SemaphoreType.DMA]
    out = call(
        functools.partial(finish_kernel, half, True),
        in_specs=[in_place] * 3,
        out_specs=in_hbm,
        out_shape=pltpu.HBM(x.shape, BF16),
        scratch_shapes=scratch,
    )(tri, gate, o_v)
    return call(
        functools.partial(finish_kernel, half, False),
        in_specs=[in_place] * 3 + [in_hbm],
        out_specs=in_hbm,
        out_shape=pltpu.HBM(x.shape, BF16),
        input_output_aliases={3: 0},
        scratch_shapes=scratch,
    )(*in_vmem(arrived), gate, o_v, pltpu.with_memory_space_constraint(out, pltpu.HBM))


def gather_plan(pair_rep, proj_weight, gate_weight, out_weight):
    rows_here, cols_here, channels = pair_rep.shape
    hidden = out_weight.shape[0]
    normed = layer_norm(pair_rep.astype(F32)).astype(BF16)
    flat_rows = normed.reshape(-1, channels)
    projected = jnp.dot(flat_rows, proj_weight, preferred_element_type=F32)
    left, right = (
        (jax.nn.sigmoid(projected[:, at : at + hidden]) * projected[:, at + hidden : at + 2 * hidden])
        .astype(BF16)
        .reshape(rows_here, cols_here, hidden)
        for at in (0, 2 * hidden)
    )
    gating = jax.nn.sigmoid(jnp.dot(flat_rows, gate_weight, preferred_element_type=F32))
    left_full = lax.all_gather(left, "col", axis=1, tiled=True)
    right_all = lax.all_gather(lax.all_gather(right, "col", axis=1, tiled=True), "row", axis=0, tiled=True)
    mine = lax.dynamic_slice_in_dim(right_all, lax.axis_index("col") * cols_here, cols_here, 0)
    combined = jnp.einsum("ikc,jkc->ijc", left_full, mine, preferred_element_type=F32)
    tri_normed = layer_norm(combined).astype(BF16).reshape(-1, hidden)
    update = jnp.dot(tri_normed, out_weight, preferred_element_type=F32) * gating
    return update.astype(BF16).reshape(rows_here, cols_here, channels)


def solution(mesh):
    def per_device(pair_rep, proj_weight, gate_weight, out_weight):
        rows_here, cols_here, channels = pair_rep.shape
        hidden = out_weight.shape[0]
        rows, cols = mesh.shape["row"], mesh.shape["col"]
        half = rows // 2
        held = 4 * hidden * (half + 3) * rows_here * cols_here + 12 * hidden * half * rows_here**2
        fits = held + 2 * half * pair_rep.size <= VMEM_BUDGET and channels == hidden
        even = cols == 2 and rows >= 4 and rows & (rows - 1) == 0 and half * rows_here == cols_here
        tiled = rows_here * cols_here % 16 == 0 and cols_here % 8 == 0 and channels % 128 == 0
        if fits and even and tiled:
            return fast_plan(mesh, pair_rep, proj_weight, gate_weight, out_weight)
        return gather_plan(pair_rep, proj_weight, gate_weight, out_weight)

    return jax.shard_map(
        per_device,
        mesh=mesh,
        in_specs=(PLACED, P(), P(), P()),
        out_specs=PLACED,
        check_vma=False,
    )
```

```python
import functools
import itertools

import jax
import jax.numpy as jnp
from jax import lax
from jax.experimental import pallas as pl
from jax.experimental.pallas import tpu as pltpu
from jax.sharding import PartitionSpec as P

F32, BF16 = jnp.float32, jnp.bfloat16
PLACED = P(("groups", "row"), "col", None)
VMEM_BUDGET = 24 * 2**20
PIECES = 3


def layer_norm(values):
    average = jnp.mean(values, axis=-1, keepdims=True)
    centered = values - average
    spread = jnp.mean(centered * centered, axis=-1, keepdims=True)
    return centered * lax.rsqrt(spread + 1e-05)


def sigmoid(values):
    return 0.5 * jnp.tanh(0.5 * values) + 0.5


def normalised(x_ref):
    x = x_ref[...].reshape(-1, x_ref.shape[-1]).astype(F32)
    return layer_norm(x).astype(BF16)


def side(normed, weight):
    both = jnp.dot(normed, weight, preferred_element_type=F32)
    hidden = both.shape[-1] // 2
    return (sigmoid(both[:, :hidden]) * both[:, hidden:]).astype(BF16).astype(F32)


def in_vmem(*arrays):
    return [pltpu.with_memory_space_constraint(a, pltpu.VMEM) for a in arrays]


def place_of(half):
    row = lax.axis_index("row")
    return lax.rem(row, half), lax.div(row, half) == lax.axis_index("col")


def put_right(half, step, x_ref, w_ref, right_ref):
    rows, hidden = x_ref.shape[0] * x_ref.shape[1], right_ref.shape[-1]
    start = pl.multiple_of((place_of(half)[0] ^ step) * rows, 8)
    right_ref[pl.ds(start, rows), :] = side(normalised(x_ref), w_ref[:, 2 * hidden :])


def own_kernel(half, x_ref, w_ref, g_ref, o_ref, left_ref, right_ref, gate_ref, w_out, g_out, o_out, x_in, sems):
    pairs = ((x_ref, x_in), (w_ref, w_out), (g_ref, g_out), (o_ref, o_out))
    copies = [pltpu.make_async_copy(a, b, sems.at[n]) for n, (a, b) in enumerate(pairs)]
    for copy in copies:
        copy.start()
    for copy in copies:
        copy.wait()
    rows, hidden = gate_ref.shape
    normed = normalised(x_in)
    left_ref[pl.ds(0, rows), :] = side(normed, w_out[:, : 2 * hidden])
    start = pl.multiple_of(place_of(half)[0] * rows, 8)
    right_ref[pl.ds(start, rows), :] = side(normed, w_out[:, 2 * hidden :])
    gate_ref[...] = sigmoid(jnp.dot(normed, g_out[...], preferred_element_type=F32))


def products(left_ref, base, right_ref, strips, places, out_ref):
    count = out_ref.shape[0]
    depth = left_ref.shape[0] // (2 * count)
    for first, at in itertools.product(range(0, count, 10), range(0, len(strips), 3)):
        rows, some = range(first, min(first + 10, count)), strips[at : at + 3]

        def body(k, sums):
            rights = [right_ref[pl.ds(s * depth + k, 8, stride=depth), :] for s in some]
            added = []
            for n, i in enumerate(rows):
                left = left_ref[pl.ds(base + i * depth + k, 1), :]
                added.append(tuple(a + left * r for a, r in zip(sums[n], rights, strict=True)))
            return tuple(added)

        zero = jnp.zeros((8, left_ref.shape[-1]), F32)
        sums = lax.fori_loop(0, depth, body, tuple(tuple(zero for _ in some) for _ in rows), unroll=4)
        for n, i in enumerate(rows):
            for place, total in zip(places[at : at + 3], sums[n], strict=True):
                out_ref[i, pl.ds(place, 8), :] = total


def strips_of(half, rows_here):
    part, total = half // 2, half * rows_here // 8
    count = min(part * rows_here // 8, total - -(-part * rows_here // 8))
    place = place_of(half)[0]
    second = lax.div(place, part)
    bounds = [(p * rows_here // 8, -(-(p + 1) * rows_here // 8)) for p in range(half)]
    held, others = max(b - a for a, b in bounds), total - count
    start = (1 - second) * count
    first = jnp.clip(lax.div((place ^ part) * rows_here, 8) - start, 0, others - held)
    early = [second * others + n for n in range(count)]
    middle = [start + jnp.where(n < first, n, n + held) for n in range(others - held)]
    late = [start + first + n for n in range(held)]
    return [[pl.multiple_of(s * 8, 8) for s in strips] for strips in (early, middle, late)]


def right_kernel(half, step, x_ref, w_ref, _, right_ref):
    put_right(half, step, x_ref, w_ref, right_ref)


def near_kernel(half, step, x_ref, w_ref, left_ref, _, right_ref, tile_ref):
    put_right(half, step, x_ref, w_ref, right_ref)
    early, _, _ = strips_of(half, tile_ref.shape[0])
    products(left_ref, 0, right_ref, early, range(0, tile_ref.shape[1], 8), tile_ref)


def far_kernel(half, far_ref, w_ref, right_ref, _, left_ref, tile_ref):
    rows, hidden = left_ref.shape[0] // 2, left_ref.shape[-1]
    left_ref[pl.ds(rows, rows), :] = side(normalised(far_ref), w_ref[:, : 2 * hidden])
    early, middle, _ = strips_of(half, tile_ref.shape[0])
    products(left_ref, rows, right_ref, early + middle, early + middle, tile_ref)


def give_kernel(half, step, x_ref, w_ref, left_ref, _r, _t, right_ref, tile_ref):
    _, _, late = strips_of(half, tile_ref.shape[0])

    @pl.when(lax.axis_index("col") == 1)
    def _():
        put_right(half, step, x_ref, w_ref, right_ref)
        products(left_ref, left_ref.shape[0] // 2, right_ref, late, late, tile_ref)


def keep_kernel(half, step, x_ref, w_ref, left_ref, own_ref, _, right_ref, last_ref, part_ref, *piece_refs):
    early, middle, late = strips_of(half, part_ref.shape[0])

    @pl.when(lax.axis_index("col") == 0)
    def _():
        put_right(half, step, x_ref, w_ref, right_ref)
        products(left_ref, left_ref.shape[0] // 2, right_ref, late, range(0, last_ref.shape[1], 8), last_ref)

    for n, s in enumerate(early):
        part_ref[:, pl.ds(s, 8), :] = own_ref[:, 8 * n : 8 * n + 8, :]
    products(left_ref, 0, right_ref, middle + late, middle + late, part_ref)
    for ref, rows in zip(piece_refs, pieces_of(part_ref.shape[0]), strict=True):
        ref[...] = part_ref[rows]


def pieces_of(count):
    ends = [count * n // PIECES for n in range(PIECES + 1)]
    return [slice(a, b) for a, b in itertools.pairwise(ends)]


def norm_kernel(half, tile_ref, last_ref, got_ref, *refs):
    tri_ref, sum_ref = refs[PIECES], refs[-1]

    @pl.when(lax.axis_index("col") == 0)
    def _():
        sum_ref[...] = tile_ref[...] + got_ref[...]
        for n, s in enumerate(strips_of(half, tri_ref.shape[0])[2]):
            sum_ref[:, pl.ds(s, 8), :] = last_ref[:, 8 * n : 8 * n + 8, :] + got_ref[:, pl.ds(s, 8), :]
        tri_ref[...] = layer_norm(sum_ref[...]).astype(BF16)


def write_update(tri, gate_ref, o_ref, out_ref, done_ref, sem):
    update = jnp.dot(tri.reshape(gate_ref.shape), o_ref[...], preferred_element_type=F32)
    done_ref[...] = (update * gate_ref[...]).astype(BF16).reshape(done_ref.shape)
    copy = pltpu.make_async_copy(done_ref, out_ref, sem)
    copy.start()
    copy.wait()


def finish_own_kernel(half, keep_ref, *refs):
    @pl.when(place_of(half)[1])
    def _():
        got_refs, (gate_ref, o_ref, out_ref, done_ref, sem) = refs[:PIECES], refs[PIECES:]
        sums = jnp.concatenate([ref[...] for ref in got_refs], axis=0)
        tri = layer_norm(keep_ref[...] + sums).astype(BF16)
        write_update(tri, gate_ref, o_ref, out_ref, done_ref, sem)


def finish_far_kernel(half, tri_ref, gate_ref, o_ref, _, out_ref, done_ref, sem):
    @pl.when(jnp.logical_not(place_of(half)[1]))
    def _():
        write_update(tri_ref[...], gate_ref, o_ref, out_ref, done_ref, sem)


def fast_plan(mesh, x, proj_weight, gate_weight, out_weight):
    rows_here, depth, _ = x.shape
    hidden = out_weight.shape[0]
    rows, half = mesh.shape["row"], mesh.shape["row"] // 2
    positions = rows_here * depth
    call = functools.partial(pl.pallas_call, compiler_params=pltpu.CompilerParams(vmem_limit_bytes=40 * 2**20))

    def from_step(step):
        return lax.ppermute(x, "row", [(i, i ^ step) for i in range(rows)])

    far = from_step(half)
    blocks = {step: from_step(step) for step in range(1, half)}
    lefts, rights = pltpu.VMEM((2 * positions, hidden), F32), pltpu.VMEM((half * positions, hidden), F32)
    brought = (x, proj_weight, gate_weight, out_weight)
    left, right, gate, w_v, _, o_v = in_vmem(
        *call(
            functools.partial(own_kernel, half),
            in_specs=[pl.BlockSpec(memory_space=pltpu.HBM)] * 4,
            out_shape=(lefts, rights, pltpu.VMEM((positions, hidden), F32), *[pltpu.VMEM(a.shape, a.dtype) for a in brought[1:]]),
            scratch_shapes=[pltpu.VMEM(x.shape, x.dtype), pltpu.SemaphoreType.DMA((4,))],
        )(*[pltpu.with_memory_space_constraint(a, pltpu.HBM) for a in brought])
    )

    def with_block(step, right):
        body = functools.partial(right_kernel, half, step)
        return call(body, out_shape=rights, input_output_aliases={2: 0})(*in_vmem(blocks[step]), w_v, *in_vmem(right))

    for step in range(half // 2 - 1, 1, -1):
        right = with_block(step, right)
    early, _, late = strips_of(half, rows_here)
    early_part, late_part = (pltpu.VMEM((rows_here, 8 * len(s), hidden), F32) for s in (early, late))
    tile_part = pltpu.VMEM((rows_here, half * rows_here, hidden), F32)
    right, own_early = in_vmem(
        *call(functools.partial(near_kernel, half, 1), out_shape=(rights, early_part), input_output_aliases={3: 0})(
            *in_vmem(blocks[1]), w_v, left, *in_vmem(right)
        )
    )
    for step in range(half - 1, half // 2, -1):
        right = with_block(step, right)
    left, far_tile = in_vmem(
        *call(functools.partial(far_kernel, half), out_shape=(lefts, tile_part), input_output_aliases={3: 0})(
            *in_vmem(far), w_v, *in_vmem(right), left
        )
    )
    last, swap = half // 2, [(0, 1), (1, 0)]
    (block,) = in_vmem(blocks[last])
    right, far_tile = in_vmem(
        *call(
            functools.partial(give_kernel, half, last), out_shape=(rights, tile_part), input_output_aliases={3: 0, 4: 1}
        )(block, w_v, left, *in_vmem(right), far_tile)
    )
    got_far = lax.ppermute(far_tile, "col", swap)
    own_pieces = [pltpu.VMEM((p.stop - p.start, *tile_part.shape[1:]), F32) for p in pieces_of(rows_here)]
    _, far_last, own_tile, *pieces = in_vmem(
        *call(
            functools.partial(keep_kernel, half, last),
            out_shape=(rights, late_part, tile_part, *own_pieces),
            input_output_aliases={4: 0},
        )(block, w_v, left, own_early, right)
    )
    tri, *pieces = in_vmem(
        *call(
            functools.partial(norm_kernel, half),
            out_shape=(pltpu.VMEM(x.shape, BF16), *own_pieces),
            input_output_aliases={3 + n: 1 + n for n in range(PIECES)},
            scratch_shapes=[pltpu.VMEM(tile_part.shape, F32)],
        )(far_tile, far_last, *in_vmem(got_far), *pieces)
    )
    pairs = [(2 * r, 2 * (r ^ half) + r // half) for r in range(rows)]
    pairs += [(2 * r + 1, 2 * r if r < half else 2 * (r ^ 1) + 1) for r in range(rows)]
    arrived = lax.ppermute(tri, ("row", "col"), pairs)
    got_own = [lax.ppermute(piece, "col", swap) for piece in pieces]
    in_place = pl.BlockSpec(memory_space=pltpu.VMEM)
    in_hbm = pl.BlockSpec(memory_space=pltpu.HBM)
    scratch = [pltpu.VMEM(x.shape, BF16), pltpu.SemaphoreType.DMA]
    out = call(
        functools.partial(finish_own_kernel, half),
        in_specs=[in_place] * (3 + PIECES),
        out_specs=in_hbm,
        out_shape=pltpu.HBM(x.shape, BF16),
        scratch_shapes=scratch,
    )(own_tile, *in_vmem(*got_own), gate, o_v)
    return call(
        functools.partial(finish_far_kernel, half),
        in_specs=[in_place] * 3 + [in_hbm],
        out_specs=in_hbm,
        out_shape=pltpu.HBM(x.shape, BF16),
        input_output_aliases={3: 0},
        scratch_shapes=scratch,
    )(*in_vmem(arrived), gate, o_v, pltpu.with_memory_space_constraint(out, pltpu.HBM))


def gather_plan(pair_rep, proj_weight, gate_weight, out_weight):
    rows_here, cols_here, channels = pair_rep.shape
    hidden = out_weight.shape[0]
    normed = layer_norm(pair_rep.astype(F32)).astype(BF16)
    flat_rows = normed.reshape(-1, channels)
    projected = jnp.dot(flat_rows, proj_weight, preferred_element_type=F32)
    left, right = (
        (jax.nn.sigmoid(projected[:, at : at + hidden]) * projected[:, at + hidden : at + 2 * hidden])
        .astype(BF16)
        .reshape(rows_here, cols_here, hidden)
        for at in (0, 2 * hidden)
    )
    gating = jax.nn.sigmoid(jnp.dot(flat_rows, gate_weight, preferred_element_type=F32))
    left_full = lax.all_gather(left, "col", axis=1, tiled=True)
    right_all = lax.all_gather(lax.all_gather(right, "col", axis=1, tiled=True), "row", axis=0, tiled=True)
    mine = lax.dynamic_slice_in_dim(right_all, lax.axis_index("col") * cols_here, cols_here, 0)
    combined = jnp.einsum("ikc,jkc->ijc", left_full, mine, preferred_element_type=F32)
    tri_normed = layer_norm(combined).astype(BF16).reshape(-1, hidden)
    update = jnp.dot(tri_normed, out_weight, preferred_element_type=F32) * gating
    return update.astype(BF16).reshape(rows_here, cols_here, channels)


def solution(mesh):
    def per_device(pair_rep, proj_weight, gate_weight, out_weight):
        rows_here, cols_here, channels = pair_rep.shape
        hidden = out_weight.shape[0]
        rows, cols = mesh.shape["row"], mesh.shape["col"]
        half = rows // 2
        held = 4 * hidden * (half + 3) * rows_here * cols_here + 12 * hidden * half * rows_here**2
        fits = held + 2 * half * pair_rep.size <= VMEM_BUDGET and channels == hidden
        even = cols == 2 and rows >= 4 and rows & (rows - 1) == 0 and half * rows_here == cols_here
        tiled = rows_here * cols_here % 16 == 0 and cols_here % 8 == 0 and channels % 128 == 0
        if fits and even and tiled:
            return fast_plan(mesh, pair_rep, proj_weight, gate_weight, out_weight)
        return gather_plan(pair_rep, proj_weight, gate_weight, out_weight)

    return jax.shard_map(
        per_device,
        mesh=mesh,
        in_specs=(PLACED, P(), P(), P()),
        out_specs=PLACED,
        check_vma=False,
    )
```

```python
import functools
import itertools

import jax
import jax.numpy as jnp
from jax import lax
from jax.experimental import pallas as pl
from jax.experimental.pallas import tpu as pltpu
from jax.sharding import PartitionSpec as P

F32, BF16 = jnp.float32, jnp.bfloat16
PLACED = P(("groups", "row"), "col", None)
VMEM_BUDGET = 24 * 2**20
PIECES = 3


def layer_norm(values):
    average = jnp.mean(values, axis=-1, keepdims=True)
    centered = values - average
    spread = jnp.mean(centered * centered, axis=-1, keepdims=True)
    return centered * lax.rsqrt(spread + 1e-05)


def sigmoid(values):
    return 0.5 * jnp.tanh(0.5 * values) + 0.5


def normalised(x_ref):
    x = x_ref[...].reshape(-1, x_ref.shape[-1]).astype(F32)
    return layer_norm(x).astype(BF16)


def side(normed, weight):
    both = jnp.dot(normed, weight, preferred_element_type=F32)
    hidden = both.shape[-1] // 2
    return (sigmoid(both[:, :hidden]) * both[:, hidden:]).astype(BF16).astype(F32)


def in_vmem(*arrays):
    return [pltpu.with_memory_space_constraint(a, pltpu.VMEM) for a in arrays]


def place_of(half):
    row = lax.axis_index("row")
    return lax.rem(row, half), lax.div(row, half) == lax.axis_index("col")


def put_right(half, step, x_ref, w_ref, right_ref):
    rows, hidden = x_ref.shape[0] * x_ref.shape[1], right_ref.shape[-1]
    start = pl.multiple_of((place_of(half)[0] ^ step) * rows, 8)
    right_ref[pl.ds(start, rows), :] = side(normalised(x_ref), w_ref[:, 2 * hidden :])


def own_kernel(half, x_ref, w_ref, g_ref, o_ref, left_ref, right_ref, gate_ref, w_out, g_out, o_out, x_in, sems):
    pairs = ((x_ref, x_in), (w_ref, w_out), (g_ref, g_out), (o_ref, o_out))
    copies = [pltpu.make_async_copy(a, b, sems.at[n]) for n, (a, b) in enumerate(pairs)]
    for copy in copies:
        copy.start()
    for copy in copies:
        copy.wait()
    rows, hidden = gate_ref.shape
    normed = normalised(x_in)
    left_ref[pl.ds(0, rows), :] = side(normed, w_out[:, : 2 * hidden])
    start = pl.multiple_of(place_of(half)[0] * rows, 8)
    right_ref[pl.ds(start, rows), :] = side(normed, w_out[:, 2 * hidden :])
    gate_ref[...] = sigmoid(jnp.dot(normed, g_out[...], preferred_element_type=F32))


def products(left_ref, base, right_ref, strips, places, out_ref):
    count = out_ref.shape[0]
    depth = left_ref.shape[0] // (2 * count)
    for first, at in itertools.product(range(0, count, 10), range(0, len(strips), 3)):
        rows, some = range(first, min(first + 10, count)), strips[at : at + 3]

        def body(k, sums):
            rights = [right_ref[pl.ds(s * depth + k, 8, stride=depth), :] for s in some]
            added = []
            for n, i in enumerate(rows):
                left = left_ref[pl.ds(base + i * depth + k, 1), :]
                added.append(tuple(a + left * r for a, r in zip(sums[n], rights, strict=True)))
            return tuple(added)

        zero = jnp.zeros((8, left_ref.shape[-1]), F32)
        sums = lax.fori_loop(0, depth, body, tuple(tuple(zero for _ in some) for _ in rows), unroll=4)
        for n, i in enumerate(rows):
            for place, total in zip(places[at : at + 3], sums[n], strict=True):
                out_ref[i, pl.ds(place, 8), :] = total


def strips_of(half, rows_here):
    part, total = half // 2, half * rows_here // 8
    count = min(part * rows_here // 8, total - -(-part * rows_here // 8))
    place = place_of(half)[0]
    second = lax.div(place, part)
    bounds = [(p * rows_here // 8, -(-(p + 1) * rows_here // 8)) for p in range(half)]
    held, others = max(b - a for a, b in bounds), total - count
    start = (1 - second) * count
    first = jnp.clip(lax.div((place ^ part) * rows_here, 8) - start, 0, others - held)
    early = [second * others + n for n in range(count)]
    middle = [start + jnp.where(n < first, n, n + held) for n in range(others - held)]
    late = [start + first + n for n in range(held)]
    return [[pl.multiple_of(s * 8, 8) for s in strips] for strips in (early, middle, late)]


def right_kernel(half, step, x_ref, w_ref, _, right_ref):
    put_right(half, step, x_ref, w_ref, right_ref)


def near_kernel(half, step, x_ref, w_ref, left_ref, _, right_ref, tile_ref):
    put_right(half, step, x_ref, w_ref, right_ref)
    early, _, _ = strips_of(half, tile_ref.shape[0])
    products(left_ref, 0, right_ref, early, range(0, tile_ref.shape[1], 8), tile_ref)


def put_far(far_ref, w_ref, left_ref):
    rows, hidden = left_ref.shape[0] // 2, left_ref.shape[-1]
    left_ref[pl.ds(rows, rows), :] = side(normalised(far_ref), w_ref[:, : 2 * hidden])


def far_kernel(half, far_ref, w_ref, right_ref, _, left_ref, tile_ref):
    early, middle, _ = strips_of(half, tile_ref.shape[0])

    @pl.when(lax.axis_index("col") == 1)
    def _():
        put_far(far_ref, w_ref, left_ref)
        products(left_ref, left_ref.shape[0] // 2, right_ref, early + middle, early + middle, tile_ref)


def give_kernel(half, step, x_ref, w_ref, left_ref, _r, _t, right_ref, tile_ref):
    _, _, late = strips_of(half, tile_ref.shape[0])

    @pl.when(lax.axis_index("col") == 1)
    def _():
        put_right(half, step, x_ref, w_ref, right_ref)
        products(left_ref, left_ref.shape[0] // 2, right_ref, late, late, tile_ref)


def late_sender(half):
    return (lax.axis_index("row") >= half) & (lax.axis_index("col") == 0)


def keep_kernel(half, step, far_ref, x_ref, w_ref, own_ref, _l, _r, left_ref, right_ref, tile_ref, *part_refs):
    early, middle, late = strips_of(half, tile_ref.shape[0])
    strips = early + middle + late

    @pl.when(lax.axis_index("col") == 0)
    def _():
        put_far(far_ref, w_ref, left_ref)
        put_right(half, step, x_ref, w_ref, right_ref)
        products(left_ref, left_ref.shape[0] // 2, right_ref, strips, strips, tile_ref)

    @pl.when(jnp.logical_not(late_sender(half)))
    def _():
        own_sums(half, left_ref, right_ref, own_ref, *part_refs)


def norm_kernel(tile_ref, got_ref, tri_ref):
    @pl.when(lax.axis_index("col") == 0)
    def _():
        tri_ref[...] = layer_norm(tile_ref[...] + got_ref[...]).astype(BF16)


def own_sums(half, left_ref, right_ref, own_ref, part_ref, *piece_refs):
    early, middle, late = strips_of(half, part_ref.shape[0])
    for n, s in enumerate(early):
        part_ref[:, pl.ds(s, 8), :] = own_ref[:, 8 * n : 8 * n + 8, :]
    products(left_ref, 0, right_ref, middle + late, middle + late, part_ref)
    for ref, rows in zip(piece_refs, pieces_of(part_ref.shape[0]), strict=True):
        ref[...] = part_ref[rows]


def own_sums_kernel(half, left_ref, right_ref, own_ref, *refs):
    @pl.when(late_sender(half))
    def _():
        own_sums(half, left_ref, right_ref, own_ref, *refs[-1 - PIECES :])


def pieces_of(count):
    ends = [count * n // PIECES for n in range(PIECES + 1)]
    return [slice(a, b) for a, b in itertools.pairwise(ends)]


def write_update(tri, gate_ref, o_ref, out_ref, done_ref, sem):
    update = jnp.dot(tri.reshape(gate_ref.shape), o_ref[...], preferred_element_type=F32)
    done_ref[...] = (update * gate_ref[...]).astype(BF16).reshape(done_ref.shape)
    copy = pltpu.make_async_copy(done_ref, out_ref, sem)
    copy.start()
    copy.wait()


def finish_own_kernel(half, keep_ref, *refs):
    @pl.when(place_of(half)[1])
    def _():
        got_refs, (gate_ref, o_ref, out_ref, done_ref, sem) = refs[:PIECES], refs[PIECES:]
        sums = jnp.concatenate([ref[...] for ref in got_refs], axis=0)
        tri = layer_norm(keep_ref[...] + sums).astype(BF16)
        write_update(tri, gate_ref, o_ref, out_ref, done_ref, sem)


def finish_far_kernel(half, tri_ref, gate_ref, o_ref, _, out_ref, done_ref, sem):
    @pl.when(jnp.logical_not(place_of(half)[1]))
    def _():
        write_update(tri_ref[...], gate_ref, o_ref, out_ref, done_ref, sem)


def fast_plan(mesh, x, proj_weight, gate_weight, out_weight):
    rows_here, depth, _ = x.shape
    hidden = out_weight.shape[0]
    rows, half = mesh.shape["row"], mesh.shape["row"] // 2
    positions = rows_here * depth
    call = functools.partial(pl.pallas_call, compiler_params=pltpu.CompilerParams(vmem_limit_bytes=40 * 2**20))

    def from_step(step):
        return lax.ppermute(x, "row", [(i, i ^ step) for i in range(rows)])

    far = from_step(half)
    blocks = {step: from_step(step) for step in range(1, half)}
    lefts, rights = pltpu.VMEM((2 * positions, hidden), F32), pltpu.VMEM((half * positions, hidden), F32)
    brought = (x, proj_weight, gate_weight, out_weight)
    left, right, gate, w_v, _, o_v = in_vmem(
        *call(
            functools.partial(own_kernel, half),
            in_specs=[pl.BlockSpec(memory_space=pltpu.HBM)] * 4,
            out_shape=(lefts, rights, pltpu.VMEM((positions, hidden), F32), *[pltpu.VMEM(a.shape, a.dtype) for a in brought[1:]]),
            scratch_shapes=[pltpu.VMEM(x.shape, x.dtype), pltpu.SemaphoreType.DMA((4,))],
        )(*[pltpu.with_memory_space_constraint(a, pltpu.HBM) for a in brought])
    )

    def with_block(step, right):
        body = functools.partial(right_kernel, half, step)
        return call(body, out_shape=rights, input_output_aliases={2: 0})(*in_vmem(blocks[step]), w_v, *in_vmem(right))

    for step in range(half // 2 - 1, 1, -1):
        right = with_block(step, right)
    early_part = pltpu.VMEM((rows_here, 8 * len(strips_of(half, rows_here)[0]), hidden), F32)
    tile_part = pltpu.VMEM((rows_here, half * rows_here, hidden), F32)
    right, own_early = in_vmem(
        *call(functools.partial(near_kernel, half, 1), out_shape=(rights, early_part), input_output_aliases={3: 0})(
            *in_vmem(blocks[1]), w_v, left, *in_vmem(right)
        )
    )
    for step in range(half - 1, half // 2, -1):
        right = with_block(step, right)
    left, far_tile = in_vmem(
        *call(functools.partial(far_kernel, half), out_shape=(lefts, tile_part), input_output_aliases={3: 0})(
            *in_vmem(far), w_v, *in_vmem(right), left
        )
    )
    last, swap = half // 2, [(0, 1), (1, 0)]
    (block,) = in_vmem(blocks[last])
    right, far_tile = in_vmem(
        *call(
            functools.partial(give_kernel, half, last), out_shape=(rights, tile_part), input_output_aliases={3: 0, 4: 1}
        )(block, w_v, left, *in_vmem(right), far_tile)
    )
    got_far = lax.ppermute(far_tile, "col", swap)
    own_pieces = [pltpu.VMEM((p.stop - p.start, *tile_part.shape[1:]), F32) for p in pieces_of(rows_here)]
    left, right, keep, *own_parts = in_vmem(
        *call(
            functools.partial(keep_kernel, half, last),
            out_shape=(lefts, rights, tile_part, tile_part, *own_pieces),
            input_output_aliases={4: 0, 5: 1},
        )(*in_vmem(far), block, w_v, own_early, left, right)
    )
    (tri,) = in_vmem(call(norm_kernel, out_shape=pltpu.VMEM(x.shape, BF16))(keep, *in_vmem(got_far)))
    pairs = [(2 * r, 2 * (r ^ half) + r // half) for r in range(rows)]
    pairs += [(2 * r + 1, 2 * r if r < half else 2 * (r ^ 1) + 1) for r in range(rows)]
    arrived = lax.ppermute(tri, ("row", "col"), pairs)
    own_tile, *pieces = in_vmem(
        *call(
            functools.partial(own_sums_kernel, half),
            out_shape=(tile_part, *own_pieces),
            input_output_aliases={4 + n: n for n in range(1 + PIECES)},
        )(left, right, own_early, tri, *own_parts)
    )
    got_own = [lax.ppermute(piece, "col", swap) for piece in pieces]
    in_place = pl.BlockSpec(memory_space=pltpu.VMEM)
    in_hbm = pl.BlockSpec(memory_space=pltpu.HBM)
    scratch = [pltpu.VMEM(x.shape, BF16), pltpu.SemaphoreType.DMA]
    out = call(
        functools.partial(finish_own_kernel, half),
        in_specs=[in_place] * (3 + PIECES),
        out_specs=in_hbm,
        out_shape=pltpu.HBM(x.shape, BF16),
        scratch_shapes=scratch,
    )(own_tile, *in_vmem(*got_own), gate, o_v)
    return call(
        functools.partial(finish_far_kernel, half),
        in_specs=[in_place] * 3 + [in_hbm],
        out_specs=in_hbm,
        out_shape=pltpu.HBM(x.shape, BF16),
        input_output_aliases={3: 0},
        scratch_shapes=scratch,
    )(*in_vmem(arrived), gate, o_v, pltpu.with_memory_space_constraint(out, pltpu.HBM))


def gather_plan(pair_rep, proj_weight, gate_weight, out_weight):
    rows_here, cols_here, channels = pair_rep.shape
    hidden = out_weight.shape[0]
    normed = layer_norm(pair_rep.astype(F32)).astype(BF16)
    flat_rows = normed.reshape(-1, channels)
    projected = jnp.dot(flat_rows, proj_weight, preferred_element_type=F32)
    left, right = (
        (jax.nn.sigmoid(projected[:, at : at + hidden]) * projected[:, at + hidden : at + 2 * hidden])
        .astype(BF16)
        .reshape(rows_here, cols_here, hidden)
        for at in (0, 2 * hidden)
    )
    gating = jax.nn.sigmoid(jnp.dot(flat_rows, gate_weight, preferred_element_type=F32))
    left_full = lax.all_gather(left, "col", axis=1, tiled=True)
    right_all = lax.all_gather(lax.all_gather(right, "col", axis=1, tiled=True), "row", axis=0, tiled=True)
    mine = lax.dynamic_slice_in_dim(right_all, lax.axis_index("col") * cols_here, cols_here, 0)
    combined = jnp.einsum("ikc,jkc->ijc", left_full, mine, preferred_element_type=F32)
    tri_normed = layer_norm(combined).astype(BF16).reshape(-1, hidden)
    update = jnp.dot(tri_normed, out_weight, preferred_element_type=F32) * gating
    return update.astype(BF16).reshape(rows_here, cols_here, channels)


def solution(mesh):
    def per_device(pair_rep, proj_weight, gate_weight, out_weight):
        rows_here, cols_here, channels = pair_rep.shape
        hidden = out_weight.shape[0]
        rows, cols = mesh.shape["row"], mesh.shape["col"]
        half = rows // 2
        held = 4 * hidden * (half + 3) * rows_here * cols_here + 12 * hidden * half * rows_here**2
        fits = held + 2 * half * pair_rep.size <= VMEM_BUDGET and channels == hidden
        even = cols == 2 and rows >= 4 and rows & (rows - 1) == 0 and half * rows_here == cols_here
        tiled = rows_here * cols_here % 16 == 0 and cols_here % 8 == 0 and channels % 128 == 0
        if fits and even and tiled:
            return fast_plan(mesh, pair_rep, proj_weight, gate_weight, out_weight)
        return gather_plan(pair_rep, proj_weight, gate_weight, out_weight)

    return jax.shard_map(
        per_device,
        mesh=mesh,
        in_specs=(PLACED, P(), P(), P()),
        out_specs=PLACED,
        check_vma=False,
    )
```

```python
import functools
import itertools

import jax
import jax.numpy as jnp
from jax import lax
from jax.experimental import pallas as pl
from jax.experimental.pallas import tpu as pltpu
from jax.sharding import PartitionSpec as P

F32, BF16 = jnp.float32, jnp.bfloat16
PLACED = P(("groups", "row"), "col", None)
VMEM_BUDGET = 24 * 2**20
PIECES = 3


def layer_norm(values):
    average = jnp.mean(values, axis=-1, keepdims=True)
    centered = values - average
    spread = jnp.mean(centered * centered, axis=-1, keepdims=True)
    return centered * lax.rsqrt(spread + 1e-05)


def sigmoid(values):
    return 0.5 * jnp.tanh(0.5 * values) + 0.5


def normalised(x_ref):
    x = x_ref[...].reshape(-1, x_ref.shape[-1]).astype(F32)
    return layer_norm(x).astype(BF16)


def side(normed, weight):
    both = jnp.dot(normed, weight, preferred_element_type=F32)
    hidden = both.shape[-1] // 2
    return (sigmoid(both[:, :hidden]) * both[:, hidden:]).astype(BF16).astype(F32)


def in_vmem(*arrays):
    return [pltpu.with_memory_space_constraint(a, pltpu.VMEM) for a in arrays]


def place_of(half):
    row = lax.axis_index("row")
    return lax.rem(row, half), lax.div(row, half) == lax.axis_index("col")


def put_right(half, step, x_ref, w_ref, right_ref):
    rows, hidden = x_ref.shape[0] * x_ref.shape[1], right_ref.shape[-1]
    start = pl.multiple_of((place_of(half)[0] ^ step) * rows, 8)
    right_ref[pl.ds(start, rows), :] = side(normalised(x_ref), w_ref[:, 2 * hidden :])


def own_kernel(half, x_ref, w_ref, g_ref, o_ref, left_ref, right_ref, gate_ref, w_out, g_out, o_out, x_in, sems):
    pairs = ((x_ref, x_in), (w_ref, w_out), (g_ref, g_out), (o_ref, o_out))
    copies = [pltpu.make_async_copy(a, b, sems.at[n]) for n, (a, b) in enumerate(pairs)]
    for copy in copies:
        copy.start()
    for copy in copies:
        copy.wait()
    rows, hidden = gate_ref.shape
    normed = normalised(x_in)
    left_ref[pl.ds(0, rows), :] = side(normed, w_out[:, : 2 * hidden])
    start = pl.multiple_of(place_of(half)[0] * rows, 8)
    right_ref[pl.ds(start, rows), :] = side(normed, w_out[:, 2 * hidden :])
    gate_ref[...] = sigmoid(jnp.dot(normed, g_out[...], preferred_element_type=F32))


def products(left_ref, base, right_ref, strips, places, out_ref):
    count = out_ref.shape[0]
    depth = left_ref.shape[0] // (2 * count)
    for first, at in itertools.product(range(0, count, 10), range(0, len(strips), 3)):
        rows, some = range(first, min(first + 10, count)), strips[at : at + 3]

        def body(k, sums):
            rights = [right_ref[pl.ds(s * depth + k, 8, stride=depth), :] for s in some]
            added = []
            for n, i in enumerate(rows):
                left = left_ref[pl.ds(base + i * depth + k, 1), :]
                added.append(tuple(a + left * r for a, r in zip(sums[n], rights, strict=True)))
            return tuple(added)

        zero = jnp.zeros((8, left_ref.shape[-1]), F32)
        sums = lax.fori_loop(0, depth, body, tuple(tuple(zero for _ in some) for _ in rows), unroll=4)
        for n, i in enumerate(rows):
            for place, total in zip(places[at : at + 3], sums[n], strict=True):
                out_ref[i, pl.ds(place, 8), :] = total


def strips_of(half, rows_here):
    part, total = half // 2, half * rows_here // 8
    count = min(part * rows_here // 8, total - -(-part * rows_here // 8))
    place = place_of(half)[0]
    second = lax.div(place, part)
    bounds = [(p * rows_here // 8, -(-(p + 1) * rows_here // 8)) for p in range(half)]
    held, others = max(b - a for a, b in bounds), total - count
    start = (1 - second) * count
    first = jnp.clip(lax.div((place ^ part) * rows_here, 8) - start, 0, others - held)
    early = [second * others + n for n in range(count)]
    middle = [start + jnp.where(n < first, n, n + held) for n in range(others - held)]
    late = [start + first + n for n in range(held)]
    return [[pl.multiple_of(s * 8, 8) for s in strips] for strips in (early, middle, late)]


def right_kernel(half, step, x_ref, w_ref, _, right_ref):
    put_right(half, step, x_ref, w_ref, right_ref)


def near_kernel(half, step, x_ref, w_ref, left_ref, _, right_ref, tile_ref):
    put_right(half, step, x_ref, w_ref, right_ref)
    early, _, _ = strips_of(half, tile_ref.shape[0])
    products(left_ref, 0, right_ref, early, range(0, tile_ref.shape[1], 8), tile_ref)


def put_far(far_ref, w_ref, left_ref):
    rows, hidden = left_ref.shape[0] // 2, left_ref.shape[-1]
    left_ref[pl.ds(rows, rows), :] = side(normalised(far_ref), w_ref[:, : 2 * hidden])


def far_kernel(half, far_ref, w_ref, right_ref, _, left_ref, tile_ref):
    early, middle, _ = strips_of(half, tile_ref.shape[0])

    @pl.when(lax.axis_index("col") == 1)
    def _():
        put_far(far_ref, w_ref, left_ref)
        products(left_ref, left_ref.shape[0] // 2, right_ref, early + middle, early + middle, tile_ref)


def give_kernel(half, step, x_ref, w_ref, left_ref, _r, _t, right_ref, tile_ref):
    _, _, late = strips_of(half, tile_ref.shape[0])

    @pl.when(lax.axis_index("col") == 1)
    def _():
        put_right(half, step, x_ref, w_ref, right_ref)
        products(left_ref, left_ref.shape[0] // 2, right_ref, late, late, tile_ref)


def late_sender(half):
    return (lax.axis_index("row") >= half) & (lax.axis_index("col") == 0)


def keep_kernel(half, step, far_ref, x_ref, w_ref, own_ref, _l, _r, left_ref, right_ref, tile_ref, *part_refs):
    early, middle, late = strips_of(half, tile_ref.shape[0])
    strips = early + middle + late

    @pl.when(lax.axis_index("col") == 0)
    def _():
        put_far(far_ref, w_ref, left_ref)
        put_right(half, step, x_ref, w_ref, right_ref)
        products(left_ref, left_ref.shape[0] // 2, right_ref, strips, strips, tile_ref)

    @pl.when(jnp.logical_not(late_sender(half)))
    def _():
        own_sums(half, left_ref, right_ref, own_ref, *part_refs)


def norm_kernel(tile_ref, got_ref, tri_ref):
    @pl.when(lax.axis_index("col") == 0)
    def _():
        tri_ref[...] = layer_norm(tile_ref[...] + got_ref[...]).astype(BF16)


def own_sums(half, left_ref, right_ref, own_ref, part_ref, *piece_refs):
    early, middle, late = strips_of(half, part_ref.shape[0])
    for n, s in enumerate(early):
        part_ref[:, pl.ds(s, 8), :] = own_ref[:, 8 * n : 8 * n + 8, :]
    products(left_ref, 0, right_ref, middle + late, middle + late, part_ref)
    for ref, rows in zip(piece_refs, pieces_of(part_ref.shape[0]), strict=True):
        ref[...] = part_ref[rows]


def own_sums_kernel(half, left_ref, right_ref, own_ref, *refs):
    @pl.when(late_sender(half))
    def _():
        own_sums(half, left_ref, right_ref, own_ref, *refs[-1 - PIECES :])


def pieces_of(count):
    ends = [count * n // PIECES for n in range(PIECES + 1)]
    return [slice(a, b) for a, b in itertools.pairwise(ends)]


def write_update(tri, gate_ref, o_ref, out_ref, done_ref, sem):
    update = jnp.dot(tri.reshape(gate_ref.shape), o_ref[...], preferred_element_type=F32)
    done_ref[...] = (update * gate_ref[...]).astype(BF16).reshape(done_ref.shape)
    copy = pltpu.make_async_copy(done_ref, out_ref, sem)
    copy.start()
    copy.wait()


def finish_own_kernel(half, keep_ref, *refs):
    @pl.when(place_of(half)[1])
    def _():
        got_refs, (gate_ref, o_ref, out_ref, done_ref, sem) = refs[:PIECES], refs[PIECES:]
        sums = jnp.concatenate([ref[...] for ref in got_refs], axis=0)
        tri = layer_norm(keep_ref[...] + sums).astype(BF16)
        write_update(tri, gate_ref, o_ref, out_ref, done_ref, sem)


def finish_far_kernel(half, tri_ref, gate_ref, o_ref, _, out_ref, done_ref, sem):
    @pl.when(jnp.logical_not(place_of(half)[1]))
    def _():
        write_update(tri_ref[...], gate_ref, o_ref, out_ref, done_ref, sem)


def fast_plan(mesh, x, proj_weight, gate_weight, out_weight):
    rows_here, depth, _ = x.shape
    hidden = out_weight.shape[0]
    rows, half = mesh.shape["row"], mesh.shape["row"] // 2
    positions = rows_here * depth
    call = functools.partial(pl.pallas_call, compiler_params=pltpu.CompilerParams(vmem_limit_bytes=40 * 2**20))

    def from_step(step):
        return lax.ppermute(x, "row", [(i, i ^ step) for i in range(rows)])

    far = from_step(half)
    blocks = {step: from_step(step) for step in range(1, half)}
    lefts, rights = pltpu.VMEM((2 * positions, hidden), F32), pltpu.VMEM((half * positions + depth, hidden), F32)
    brought = (x, proj_weight, gate_weight, out_weight)
    left, right, gate, w_v, _, o_v = in_vmem(
        *call(
            functools.partial(own_kernel, half),
            in_specs=[pl.BlockSpec(memory_space=pltpu.HBM)] * 4,
            out_shape=(lefts, rights, pltpu.VMEM((positions, hidden), F32), *[pltpu.VMEM(a.shape, a.dtype) for a in brought[1:]]),
            scratch_shapes=[pltpu.VMEM(x.shape, x.dtype), pltpu.SemaphoreType.DMA((4,))],
        )(*[pltpu.with_memory_space_constraint(a, pltpu.HBM) for a in brought])
    )

    def with_block(step, right):
        body = functools.partial(right_kernel, half, step)
        return call(body, out_shape=rights, input_output_aliases={2: 0})(*in_vmem(blocks[step]), w_v, *in_vmem(right))

    for step in range(half // 2 - 1, 1, -1):
        right = with_block(step, right)
    early_part = pltpu.VMEM((rows_here, 8 * len(strips_of(half, rows_here)[0]), hidden), F32)
    tile_part = pltpu.VMEM((rows_here, half * rows_here, hidden), F32)
    right, own_early = in_vmem(
        *call(functools.partial(near_kernel, half, 1), out_shape=(rights, early_part), input_output_aliases={3: 0})(
            *in_vmem(blocks[1]), w_v, left, *in_vmem(right)
        )
    )
    for step in range(half - 1, half // 2, -1):
        right = with_block(step, right)
    left, far_tile = in_vmem(
        *call(functools.partial(far_kernel, half), out_shape=(lefts, tile_part), input_output_aliases={3: 0})(
            *in_vmem(far), w_v, *in_vmem(right), left
        )
    )
    last, swap = half // 2, [(0, 1), (1, 0)]
    (block,) = in_vmem(blocks[last])
    right, far_tile = in_vmem(
        *call(
            functools.partial(give_kernel, half, last), out_shape=(rights, tile_part), input_output_aliases={3: 0, 4: 1}
        )(block, w_v, left, *in_vmem(right), far_tile)
    )
    got_far = lax.ppermute(far_tile, "col", swap)
    own_pieces = [pltpu.VMEM((p.stop - p.start, *tile_part.shape[1:]), F32) for p in pieces_of(rows_here)]
    left, right, keep, *own_parts = in_vmem(
        *call(
            functools.partial(keep_kernel, half, last),
            out_shape=(lefts, rights, tile_part, tile_part, *own_pieces),
            input_output_aliases={4: 0, 5: 1},
        )(*in_vmem(far), block, w_v, own_early, left, right)
    )
    (tri,) = in_vmem(call(norm_kernel, out_shape=pltpu.VMEM(x.shape, BF16))(keep, *in_vmem(got_far)))
    pairs = [(2 * r, 2 * (r ^ half) + r // half) for r in range(rows)]
    pairs += [(2 * r + 1, 2 * r if r < half else 2 * (r ^ 1) + 1) for r in range(rows)]
    arrived = lax.ppermute(tri, ("row", "col"), pairs)
    own_tile, *pieces = in_vmem(
        *call(
            functools.partial(own_sums_kernel, half),
            out_shape=(tile_part, *own_pieces),
            input_output_aliases={4 + n: n for n in range(1 + PIECES)},
        )(left, right, own_early, tri, *own_parts)
    )
    got_own = [lax.ppermute(piece, "col", swap) for piece in pieces]
    in_place = pl.BlockSpec(memory_space=pltpu.VMEM)
    in_hbm = pl.BlockSpec(memory_space=pltpu.HBM)
    scratch = [pltpu.VMEM(x.shape, BF16), pltpu.SemaphoreType.DMA]
    out = call(
        functools.partial(finish_own_kernel, half),
        in_specs=[in_place] * (3 + PIECES),
        out_specs=in_hbm,
        out_shape=pltpu.HBM(x.shape, BF16),
        scratch_shapes=scratch,
    )(own_tile, *in_vmem(*got_own), gate, o_v)
    return call(
        functools.partial(finish_far_kernel, half),
        in_specs=[in_place] * 3 + [in_hbm],
        out_specs=in_hbm,
        out_shape=pltpu.HBM(x.shape, BF16),
        input_output_aliases={3: 0},
        scratch_shapes=scratch,
    )(*in_vmem(arrived), gate, o_v, pltpu.with_memory_space_constraint(out, pltpu.HBM))


def gather_plan(pair_rep, proj_weight, gate_weight, out_weight):
    rows_here, cols_here, channels = pair_rep.shape
    hidden = out_weight.shape[0]
    normed = layer_norm(pair_rep.astype(F32)).astype(BF16)
    flat_rows = normed.reshape(-1, channels)
    projected = jnp.dot(flat_rows, proj_weight, preferred_element_type=F32)
    left, right = (
        (jax.nn.sigmoid(projected[:, at : at + hidden]) * projected[:, at + hidden : at + 2 * hidden])
        .astype(BF16)
        .reshape(rows_here, cols_here, hidden)
        for at in (0, 2 * hidden)
    )
    gating = jax.nn.sigmoid(jnp.dot(flat_rows, gate_weight, preferred_element_type=F32))
    left_full = lax.all_gather(left, "col", axis=1, tiled=True)
    right_all = lax.all_gather(lax.all_gather(right, "col", axis=1, tiled=True), "row", axis=0, tiled=True)
    mine = lax.dynamic_slice_in_dim(right_all, lax.axis_index("col") * cols_here, cols_here, 0)
    combined = jnp.einsum("ikc,jkc->ijc", left_full, mine, preferred_element_type=F32)
    tri_normed = layer_norm(combined).astype(BF16).reshape(-1, hidden)
    update = jnp.dot(tri_normed, out_weight, preferred_element_type=F32) * gating
    return update.astype(BF16).reshape(rows_here, cols_here, channels)


def solution(mesh):
    def per_device(pair_rep, proj_weight, gate_weight, out_weight):
        rows_here, cols_here, channels = pair_rep.shape
        hidden = out_weight.shape[0]
        rows, cols = mesh.shape["row"], mesh.shape["col"]
        half = rows // 2
        held = 4 * hidden * (half + 3) * rows_here * cols_here + 12 * hidden * half * rows_here**2
        fits = held + 2 * half * pair_rep.size <= VMEM_BUDGET and channels == hidden
        even = cols == 2 and rows >= 4 and rows & (rows - 1) == 0 and half * rows_here == cols_here
        tiled = rows_here * cols_here % 16 == 0 and cols_here % 8 == 0 and channels % 128 == 0
        if fits and even and tiled:
            return fast_plan(mesh, pair_rep, proj_weight, gate_weight, out_weight)
        return gather_plan(pair_rep, proj_weight, gate_weight, out_weight)

    return jax.shard_map(
        per_device,
        mesh=mesh,
        in_specs=(PLACED, P(), P(), P()),
        out_specs=PLACED,
        check_vma=False,
    )
```

```python
import functools
import itertools

import jax
import jax.numpy as jnp
from jax import lax
from jax.experimental import pallas as pl
from jax.experimental.pallas import tpu as pltpu
from jax.sharding import PartitionSpec as P

F32, BF16 = jnp.float32, jnp.bfloat16
PLACED = P(("groups", "row"), "col", None)
VMEM_BUDGET = 24 * 2**20
PIECES = 3


def layer_norm(values):
    average = jnp.mean(values, axis=-1, keepdims=True)
    centered = values - average
    spread = jnp.mean(centered * centered, axis=-1, keepdims=True)
    return centered * lax.rsqrt(spread + 1e-05)


def sigmoid(values):
    return 0.5 * jnp.tanh(0.5 * values) + 0.5


def normalised(x_ref):
    x = x_ref[...].reshape(-1, x_ref.shape[-1]).astype(F32)
    return layer_norm(x).astype(BF16)


def side(normed, weight):
    both = jnp.dot(normed, weight, preferred_element_type=F32)
    hidden = both.shape[-1] // 2
    return (sigmoid(both[:, :hidden]) * both[:, hidden:]).astype(BF16).astype(F32)


def in_vmem(*arrays):
    return [pltpu.with_memory_space_constraint(a, pltpu.VMEM) for a in arrays]


def place_of(half):
    row = lax.axis_index("row")
    return lax.rem(row, half), lax.div(row, half) == lax.axis_index("col")


def put_right(half, step, x_ref, w_ref, right_ref):
    rows, hidden = x_ref.shape[0] * x_ref.shape[1], right_ref.shape[-1]
    start = pl.multiple_of((place_of(half)[0] ^ step) * rows, 8)
    right_ref[pl.ds(start, rows), :] = side(normalised(x_ref), w_ref[:, 2 * hidden :])


def own_kernel(half, x_ref, w_ref, g_ref, o_ref, left_ref, right_ref, gate_ref, w_out, g_out, o_out, x_in, sems):
    pairs = ((x_ref, x_in), (w_ref, w_out), (g_ref, g_out), (o_ref, o_out))
    copies = [pltpu.make_async_copy(a, b, sems.at[n]) for n, (a, b) in enumerate(pairs)]
    for copy in copies:
        copy.start()
    for copy in copies:
        copy.wait()
    rows, hidden = gate_ref.shape
    normed = normalised(x_in)
    left_ref[pl.ds(0, rows), :] = side(normed, w_out[:, : 2 * hidden])
    start = pl.multiple_of(place_of(half)[0] * rows, 8)
    right_ref[pl.ds(start, rows), :] = side(normed, w_out[:, 2 * hidden :])
    gate_ref[...] = sigmoid(jnp.dot(normed, g_out[...], preferred_element_type=F32))


def products(left_ref, base, right_ref, strips, places, out_ref):
    count = out_ref.shape[0]
    depth = left_ref.shape[0] // (2 * count)
    for first, at in itertools.product(range(0, count, 10), range(0, len(strips), 3)):
        rows, some = range(first, min(first + 10, count)), strips[at : at + 3]

        def body(k, sums):
            rights = [right_ref[pl.ds(s * depth + k, 8, stride=depth), :] for s in some]
            added = []
            for n, i in enumerate(rows):
                left = left_ref[pl.ds(base + i * depth + k, 1), :]
                added.append(tuple(a + left * r for a, r in zip(sums[n], rights, strict=True)))
            return tuple(added)

        zero = jnp.zeros((8, left_ref.shape[-1]), F32)
        sums = lax.fori_loop(0, depth, body, tuple(tuple(zero for _ in some) for _ in rows), unroll=20)
        for n, i in enumerate(rows):
            for place, total in zip(places[at : at + 3], sums[n], strict=True):
                out_ref[i, pl.ds(place, 8), :] = total


def strips_of(half, rows_here):
    part, total = half // 2, half * rows_here // 8
    count = min(part * rows_here // 8, total - -(-part * rows_here // 8))
    place = place_of(half)[0]
    second = lax.div(place, part)
    bounds = [(p * rows_here // 8, -(-(p + 1) * rows_here // 8)) for p in range(half)]
    held, others = max(b - a for a, b in bounds), total - count
    start = (1 - second) * count
    first = jnp.clip(lax.div((place ^ part) * rows_here, 8) - start, 0, others - held)
    early = [second * others + n for n in range(count)]
    middle = [start + jnp.where(n < first, n, n + held) for n in range(others - held)]
    late = [start + first + n for n in range(held)]
    return [[pl.multiple_of(s * 8, 8) for s in strips] for strips in (early, middle, late)]


def right_kernel(half, step, x_ref, w_ref, _, right_ref):
    put_right(half, step, x_ref, w_ref, right_ref)


def near_kernel(half, step, x_ref, w_ref, left_ref, _, right_ref, tile_ref):
    put_right(half, step, x_ref, w_ref, right_ref)
    early, _, _ = strips_of(half, tile_ref.shape[0])
    products(left_ref, 0, right_ref, early, range(0, tile_ref.shape[1], 8), tile_ref)


def put_far(far_ref, w_ref, left_ref):
    rows, hidden = left_ref.shape[0] // 2, left_ref.shape[-1]
    left_ref[pl.ds(rows, rows), :] = side(normalised(far_ref), w_ref[:, : 2 * hidden])


def far_kernel(half, far_ref, w_ref, right_ref, _, left_ref, tile_ref):
    early, middle, _ = strips_of(half, tile_ref.shape[0])

    @pl.when(lax.axis_index("col") == 1)
    def _():
        put_far(far_ref, w_ref, left_ref)
        products(left_ref, left_ref.shape[0] // 2, right_ref, early + middle, early + middle, tile_ref)


def give_kernel(half, step, x_ref, w_ref, left_ref, _r, _t, right_ref, tile_ref):
    _, _, late = strips_of(half, tile_ref.shape[0])

    @pl.when(lax.axis_index("col") == 1)
    def _():
        put_right(half, step, x_ref, w_ref, right_ref)
        products(left_ref, left_ref.shape[0] // 2, right_ref, late, late, tile_ref)


def late_sender(half):
    return (lax.axis_index("row") >= half) & (lax.axis_index("col") == 0)


def keep_kernel(half, step, far_ref, x_ref, w_ref, own_ref, _l, _r, left_ref, right_ref, tile_ref, *part_refs):
    early, middle, late = strips_of(half, tile_ref.shape[0])
    strips = early + middle + late

    @pl.when(lax.axis_index("col") == 0)
    def _():
        put_far(far_ref, w_ref, left_ref)
        put_right(half, step, x_ref, w_ref, right_ref)
        products(left_ref, left_ref.shape[0] // 2, right_ref, strips, strips, tile_ref)

    @pl.when(jnp.logical_not(late_sender(half)))
    def _():
        own_sums(half, left_ref, right_ref, own_ref, *part_refs)


def norm_kernel(tile_ref, got_ref, tri_ref):
    @pl.when(lax.axis_index("col") == 0)
    def _():
        tri_ref[...] = layer_norm(tile_ref[...] + got_ref[...]).astype(BF16)


def own_sums(half, left_ref, right_ref, own_ref, part_ref, *piece_refs):
    early, middle, late = strips_of(half, part_ref.shape[0])
    for n, s in enumerate(early):
        part_ref[:, pl.ds(s, 8), :] = own_ref[:, 8 * n : 8 * n + 8, :]
    products(left_ref, 0, right_ref, middle + late, middle + late, part_ref)
    for ref, rows in zip(piece_refs, pieces_of(part_ref.shape[0]), strict=True):
        ref[...] = part_ref[rows]


def own_sums_kernel(half, left_ref, right_ref, own_ref, *refs):
    @pl.when(late_sender(half))
    def _():
        own_sums(half, left_ref, right_ref, own_ref, *refs[-1 - PIECES :])


def pieces_of(count):
    ends = [count * n // PIECES for n in range(PIECES + 1)]
    return [slice(a, b) for a, b in itertools.pairwise(ends)]


def write_update(tri, gate_ref, o_ref, out_ref, done_ref, sem):
    update = jnp.dot(tri.reshape(gate_ref.shape), o_ref[...], preferred_element_type=F32)
    done_ref[...] = (update * gate_ref[...]).astype(BF16).reshape(done_ref.shape)
    copy = pltpu.make_async_copy(done_ref, out_ref, sem)
    copy.start()
    copy.wait()


def finish_own_kernel(half, keep_ref, *refs):
    @pl.when(place_of(half)[1])
    def _():
        got_refs, (gate_ref, o_ref, out_ref, done_ref, sem) = refs[:PIECES], refs[PIECES:]
        sums = jnp.concatenate([ref[...] for ref in got_refs], axis=0)
        tri = layer_norm(keep_ref[...] + sums).astype(BF16)
        write_update(tri, gate_ref, o_ref, out_ref, done_ref, sem)


def finish_far_kernel(half, tri_ref, gate_ref, o_ref, _, out_ref, done_ref, sem):
    @pl.when(jnp.logical_not(place_of(half)[1]))
    def _():
        write_update(tri_ref[...], gate_ref, o_ref, out_ref, done_ref, sem)


def fast_plan(mesh, x, proj_weight, gate_weight, out_weight):
    rows_here, depth, _ = x.shape
    hidden = out_weight.shape[0]
    rows, half = mesh.shape["row"], mesh.shape["row"] // 2
    positions = rows_here * depth
    call = functools.partial(pl.pallas_call, compiler_params=pltpu.CompilerParams(vmem_limit_bytes=40 * 2**20))

    def from_step(step):
        return lax.ppermute(x, "row", [(i, i ^ step) for i in range(rows)])

    far = from_step(half)
    blocks = {step: from_step(step) for step in range(1, half)}
    lefts, rights = pltpu.VMEM((2 * positions, hidden), F32), pltpu.VMEM((half * positions + depth, hidden), F32)
    brought = (x, proj_weight, gate_weight, out_weight)
    left, right, gate, w_v, _, o_v = in_vmem(
        *call(
            functools.partial(own_kernel, half),
            in_specs=[pl.BlockSpec(memory_space=pltpu.HBM)] * 4,
            out_shape=(lefts, rights, pltpu.VMEM((positions, hidden), F32), *[pltpu.VMEM(a.shape, a.dtype) for a in brought[1:]]),
            scratch_shapes=[pltpu.VMEM(x.shape, x.dtype), pltpu.SemaphoreType.DMA((4,))],
        )(*[pltpu.with_memory_space_constraint(a, pltpu.HBM) for a in brought])
    )

    def with_block(step, right):
        body = functools.partial(right_kernel, half, step)
        return call(body, out_shape=rights, input_output_aliases={2: 0})(*in_vmem(blocks[step]), w_v, *in_vmem(right))

    for step in range(half // 2 - 1, 1, -1):
        right = with_block(step, right)
    early_part = pltpu.VMEM((rows_here, 8 * len(strips_of(half, rows_here)[0]), hidden), F32)
    tile_part = pltpu.VMEM((rows_here, half * rows_here, hidden), F32)
    right, own_early = in_vmem(
        *call(functools.partial(near_kernel, half, 1), out_shape=(rights, early_part), input_output_aliases={3: 0})(
            *in_vmem(blocks[1]), w_v, left, *in_vmem(right)
        )
    )
    for step in range(half - 1, half // 2, -1):
        right = with_block(step, right)
    left, far_tile = in_vmem(
        *call(functools.partial(far_kernel, half), out_shape=(lefts, tile_part), input_output_aliases={3: 0})(
            *in_vmem(far), w_v, *in_vmem(right), left
        )
    )
    last, swap = half // 2, [(0, 1), (1, 0)]
    (block,) = in_vmem(blocks[last])
    right, far_tile = in_vmem(
        *call(
            functools.partial(give_kernel, half, last), out_shape=(rights, tile_part), input_output_aliases={3: 0, 4: 1}
        )(block, w_v, left, *in_vmem(right), far_tile)
    )
    got_far = lax.ppermute(far_tile, "col", swap)
    own_pieces = [pltpu.VMEM((p.stop - p.start, *tile_part.shape[1:]), F32) for p in pieces_of(rows_here)]
    left, right, keep, *own_parts = in_vmem(
        *call(
            functools.partial(keep_kernel, half, last),
            out_shape=(lefts, rights, tile_part, tile_part, *own_pieces),
            input_output_aliases={4: 0, 5: 1},
        )(*in_vmem(far), block, w_v, own_early, left, right)
    )
    (tri,) = in_vmem(call(norm_kernel, out_shape=pltpu.VMEM(x.shape, BF16))(keep, *in_vmem(got_far)))
    pairs = [(2 * r, 2 * (r ^ half) + r // half) for r in range(rows)]
    pairs += [(2 * r + 1, 2 * r if r < half else 2 * (r ^ 1) + 1) for r in range(rows)]
    arrived = lax.ppermute(tri, ("row", "col"), pairs)
    own_tile, *pieces = in_vmem(
        *call(
            functools.partial(own_sums_kernel, half),
            out_shape=(tile_part, *own_pieces),
            input_output_aliases={4 + n: n for n in range(1 + PIECES)},
        )(left, right, own_early, tri, *own_parts)
    )
    got_own = [lax.ppermute(piece, "col", swap) for piece in pieces]
    in_place = pl.BlockSpec(memory_space=pltpu.VMEM)
    in_hbm = pl.BlockSpec(memory_space=pltpu.HBM)
    scratch = [pltpu.VMEM(x.shape, BF16), pltpu.SemaphoreType.DMA]
    out = call(
        functools.partial(finish_own_kernel, half),
        in_specs=[in_place] * (3 + PIECES),
        out_specs=in_hbm,
        out_shape=pltpu.HBM(x.shape, BF16),
        scratch_shapes=scratch,
    )(own_tile, *in_vmem(*got_own), gate, o_v)
    return call(
        functools.partial(finish_far_kernel, half),
        in_specs=[in_place] * 3 + [in_hbm],
        out_specs=in_hbm,
        out_shape=pltpu.HBM(x.shape, BF16),
        input_output_aliases={3: 0},
        scratch_shapes=scratch,
    )(*in_vmem(arrived), gate, o_v, pltpu.with_memory_space_constraint(out, pltpu.HBM))


def gather_plan(pair_rep, proj_weight, gate_weight, out_weight):
    rows_here, cols_here, channels = pair_rep.shape
    hidden = out_weight.shape[0]
    normed = layer_norm(pair_rep.astype(F32)).astype(BF16)
    flat_rows = normed.reshape(-1, channels)
    projected = jnp.dot(flat_rows, proj_weight, preferred_element_type=F32)
    left, right = (
        (jax.nn.sigmoid(projected[:, at : at + hidden]) * projected[:, at + hidden : at + 2 * hidden])
        .astype(BF16)
        .reshape(rows_here, cols_here, hidden)
        for at in (0, 2 * hidden)
    )
    gating = jax.nn.sigmoid(jnp.dot(flat_rows, gate_weight, preferred_element_type=F32))
    left_full = lax.all_gather(left, "col", axis=1, tiled=True)
    right_all = lax.all_gather(lax.all_gather(right, "col", axis=1, tiled=True), "row", axis=0, tiled=True)
    mine = lax.dynamic_slice_in_dim(right_all, lax.axis_index("col") * cols_here, cols_here, 0)
    combined = jnp.einsum("ikc,jkc->ijc", left_full, mine, preferred_element_type=F32)
    tri_normed = layer_norm(combined).astype(BF16).reshape(-1, hidden)
    update = jnp.dot(tri_normed, out_weight, preferred_element_type=F32) * gating
    return update.astype(BF16).reshape(rows_here, cols_here, channels)


def solution(mesh):
    def per_device(pair_rep, proj_weight, gate_weight, out_weight):
        rows_here, cols_here, channels = pair_rep.shape
        hidden = out_weight.shape[0]
        rows, cols = mesh.shape["row"], mesh.shape["col"]
        half = rows // 2
        held = 4 * hidden * (half + 3) * rows_here * cols_here + 12 * hidden * half * rows_here**2
        fits = held + 2 * half * pair_rep.size <= VMEM_BUDGET and channels == hidden
        even = cols == 2 and rows >= 4 and rows & (rows - 1) == 0 and half * rows_here == cols_here
        tiled = rows_here * cols_here % 16 == 0 and cols_here % 8 == 0 and channels % 128 == 0
        if fits and even and tiled:
            return fast_plan(mesh, pair_rep, proj_weight, gate_weight, out_weight)
        return gather_plan(pair_rep, proj_weight, gate_weight, out_weight)

    return jax.shard_map(
        per_device,
        mesh=mesh,
        in_specs=(PLACED, P(), P(), P()),
        out_specs=PLACED,
        check_vma=False,
    )
```

```python
import functools
import itertools

import jax
import jax.numpy as jnp
from jax import lax
from jax.experimental import pallas as pl
from jax.experimental.pallas import tpu as pltpu
from jax.sharding import PartitionSpec as P

F32, BF16 = jnp.float32, jnp.bfloat16
PLACED = P(("groups", "row"), "col", None)
VMEM_BUDGET = 24 * 2**20
PIECES = 3


def layer_norm(values):
    average = jnp.mean(values, axis=-1, keepdims=True)
    centered = values - average
    spread = jnp.mean(centered * centered, axis=-1, keepdims=True)
    return centered * lax.rsqrt(spread + 1e-05)


def sigmoid(values):
    return 0.5 * jnp.tanh(0.5 * values) + 0.5


def normalised(x_ref):
    x = x_ref[...].reshape(-1, x_ref.shape[-1]).astype(F32)
    return layer_norm(x).astype(BF16)


def side(normed, weight):
    both = jnp.dot(normed, weight, preferred_element_type=F32)
    hidden = both.shape[-1] // 2
    return (sigmoid(both[:, :hidden]) * both[:, hidden:]).astype(BF16).astype(F32)


def in_vmem(*arrays):
    return [pltpu.with_memory_space_constraint(a, pltpu.VMEM) for a in arrays]


def place_of(half):
    row = lax.axis_index("row")
    return lax.rem(row, half), lax.div(row, half) == lax.axis_index("col")


def put_right(half, step, x_ref, w_ref, right_ref):
    rows, hidden = x_ref.shape[0] * x_ref.shape[1], right_ref.shape[-1]
    start = pl.multiple_of((place_of(half)[0] ^ step) * rows, 8)
    right_ref[pl.ds(start, rows), :] = side(normalised(x_ref), w_ref[:, 2 * hidden :])


def own_kernel(half, x_ref, w_ref, g_ref, o_ref, left_ref, right_ref, gate_ref, w_out, g_out, o_out, x_in, sems):
    pairs = ((x_ref, x_in), (w_ref, w_out), (g_ref, g_out), (o_ref, o_out))
    copies = [pltpu.make_async_copy(a, b, sems.at[n]) for n, (a, b) in enumerate(pairs)]
    for copy in copies:
        copy.start()
    for copy in copies:
        copy.wait()
    rows, hidden = gate_ref.shape
    normed = normalised(x_in)
    left_ref[pl.ds(0, rows), :] = side(normed, w_out[:, : 2 * hidden])
    start = pl.multiple_of(place_of(half)[0] * rows, 8)
    right_ref[pl.ds(start, rows), :] = side(normed, w_out[:, 2 * hidden :])
    gate_ref[...] = sigmoid(jnp.dot(normed, g_out[...], preferred_element_type=F32))


def products(left_ref, base, right_ref, strips, places, out_ref):
    count = out_ref.shape[0]
    depth = left_ref.shape[0] // (2 * count)
    for first, at in itertools.product(range(0, count, 10), range(0, len(strips), 3)):
        rows, some = range(first, min(first + 10, count)), strips[at : at + 3]

        def body(k, sums):
            rights = [right_ref[pl.ds(s * depth + k, 8, stride=depth), :] for s in some]
            added = []
            for n, i in enumerate(rows):
                left = left_ref[pl.ds(base + i * depth + k, 1), :]
                added.append(tuple(a + left * r for a, r in zip(sums[n], rights, strict=True)))
            return tuple(added)

        zero = jnp.zeros((8, left_ref.shape[-1]), F32)
        sums = lax.fori_loop(0, depth, body, tuple(tuple(zero for _ in some) for _ in rows), unroll=20)
        for n, i in enumerate(rows):
            for place, total in zip(places[at : at + 3], sums[n], strict=True):
                out_ref[i, pl.ds(place, 8), :] = total


def strips_of(half, rows_here):
    part, total = half // 2, half * rows_here // 8
    count = min(part * rows_here // 8, total - -(-part * rows_here // 8))
    place = place_of(half)[0]
    second = lax.div(place, part)
    bounds = [(p * rows_here // 8, -(-(p + 1) * rows_here // 8)) for p in range(half)]
    held, others = max(b - a for a, b in bounds), total - count
    start = (1 - second) * count
    first = jnp.clip(lax.div((place ^ part) * rows_here, 8) - start, 0, others - held)
    early = [second * others + n for n in range(count)]
    middle = [start + jnp.where(n < first, n, n + held) for n in range(others - held)]
    late = [start + first + n for n in range(held)]
    return [[pl.multiple_of(s * 8, 8) for s in strips] for strips in (early, middle, late)]


def right_kernel(half, step, x_ref, w_ref, _, right_ref):
    put_right(half, step, x_ref, w_ref, right_ref)


def near_kernel(half, step, x_ref, w_ref, left_ref, _, right_ref, tile_ref):
    put_right(half, step, x_ref, w_ref, right_ref)
    early, _, _ = strips_of(half, tile_ref.shape[0])
    products(left_ref, 0, right_ref, early, range(0, tile_ref.shape[1], 8), tile_ref)


def put_far(far_ref, w_ref, left_ref):
    rows, hidden = left_ref.shape[0] // 2, left_ref.shape[-1]
    left_ref[pl.ds(rows, rows), :] = side(normalised(far_ref), w_ref[:, : 2 * hidden])


def far_kernel(half, far_ref, w_ref, right_ref, _, left_ref, tile_ref):
    early, middle, _ = strips_of(half, tile_ref.shape[0])

    @pl.when(jnp.logical_not(late_sender(half)))
    def _():
        put_far(far_ref, w_ref, left_ref)

    @pl.when(lax.axis_index("col") == 1)
    def _():
        products(left_ref, left_ref.shape[0] // 2, right_ref, early + middle, early + middle, tile_ref)


def give_kernel(half, step, x_ref, w_ref, left_ref, _r, _t, right_ref, tile_ref):
    _, _, late = strips_of(half, tile_ref.shape[0])

    @pl.when(lax.axis_index("col") == 1)
    def _():
        put_right(half, step, x_ref, w_ref, right_ref)
        products(left_ref, left_ref.shape[0] // 2, right_ref, late, late, tile_ref)


def late_sender(half):
    return (lax.axis_index("row") >= half) & (lax.axis_index("col") == 0)


def keep_kernel(half, step, far_ref, x_ref, w_ref, own_ref, _l, _r, left_ref, right_ref, tile_ref, *part_refs):
    early, middle, late = strips_of(half, tile_ref.shape[0])
    strips = early + middle + late

    @pl.when(late_sender(half))
    def _():
        put_far(far_ref, w_ref, left_ref)

    @pl.when(lax.axis_index("col") == 0)
    def _():
        put_right(half, step, x_ref, w_ref, right_ref)
        products(left_ref, left_ref.shape[0] // 2, right_ref, strips, strips, tile_ref)

    @pl.when(jnp.logical_not(late_sender(half)))
    def _():
        own_sums(half, left_ref, right_ref, own_ref, *part_refs)


def norm_kernel(tile_ref, got_ref, tri_ref):
    @pl.when(lax.axis_index("col") == 0)
    def _():
        tri_ref[...] = layer_norm(tile_ref[...] + got_ref[...]).astype(BF16)


def own_sums(half, left_ref, right_ref, own_ref, part_ref, *piece_refs):
    early, middle, late = strips_of(half, part_ref.shape[0])
    for n, s in enumerate(early):
        part_ref[:, pl.ds(s, 8), :] = own_ref[:, 8 * n : 8 * n + 8, :]
    products(left_ref, 0, right_ref, middle + late, middle + late, part_ref)
    for ref, rows in zip(piece_refs, pieces_of(part_ref.shape[0]), strict=True):
        ref[...] = part_ref[rows]


def own_sums_kernel(half, left_ref, right_ref, own_ref, *refs):
    @pl.when(late_sender(half))
    def _():
        own_sums(half, left_ref, right_ref, own_ref, *refs[-1 - PIECES :])


def pieces_of(count):
    ends = [count * n // PIECES for n in range(PIECES + 1)]
    return [slice(a, b) for a, b in itertools.pairwise(ends)]


def write_update(tri, gate_ref, o_ref, out_ref, done_ref, sem):
    update = jnp.dot(tri.reshape(gate_ref.shape), o_ref[...], preferred_element_type=F32)
    done_ref[...] = (update * gate_ref[...]).astype(BF16).reshape(done_ref.shape)
    copy = pltpu.make_async_copy(done_ref, out_ref, sem)
    copy.start()
    copy.wait()


def finish_own_kernel(half, keep_ref, *refs):
    @pl.when(place_of(half)[1])
    def _():
        got_refs, (gate_ref, o_ref, out_ref, done_ref, sem) = refs[:PIECES], refs[PIECES:]
        sums = jnp.concatenate([ref[...] for ref in got_refs], axis=0)
        tri = layer_norm(keep_ref[...] + sums).astype(BF16)
        write_update(tri, gate_ref, o_ref, out_ref, done_ref, sem)


def finish_far_kernel(half, tri_ref, gate_ref, o_ref, _, out_ref, done_ref, sem):
    @pl.when(jnp.logical_not(place_of(half)[1]))
    def _():
        write_update(tri_ref[...], gate_ref, o_ref, out_ref, done_ref, sem)


def fast_plan(mesh, x, proj_weight, gate_weight, out_weight):
    rows_here, depth, _ = x.shape
    hidden = out_weight.shape[0]
    rows, half = mesh.shape["row"], mesh.shape["row"] // 2
    positions = rows_here * depth
    call = functools.partial(pl.pallas_call, compiler_params=pltpu.CompilerParams(vmem_limit_bytes=40 * 2**20))

    def from_step(step):
        return lax.ppermute(x, "row", [(i, i ^ step) for i in range(rows)])

    far = from_step(half)
    blocks = {step: from_step(step) for step in range(1, half)}
    lefts, rights = pltpu.VMEM((2 * positions, hidden), F32), pltpu.VMEM((half * positions + depth, hidden), F32)
    brought = (x, proj_weight, gate_weight, out_weight)
    left, right, gate, w_v, _, o_v = in_vmem(
        *call(
            functools.partial(own_kernel, half),
            in_specs=[pl.BlockSpec(memory_space=pltpu.HBM)] * 4,
            out_shape=(lefts, rights, pltpu.VMEM((positions, hidden), F32), *[pltpu.VMEM(a.shape, a.dtype) for a in brought[1:]]),
            scratch_shapes=[pltpu.VMEM(x.shape, x.dtype), pltpu.SemaphoreType.DMA((4,))],
        )(*[pltpu.with_memory_space_constraint(a, pltpu.HBM) for a in brought])
    )

    def with_block(step, right):
        body = functools.partial(right_kernel, half, step)
        return call(body, out_shape=rights, input_output_aliases={2: 0})(*in_vmem(blocks[step]), w_v, *in_vmem(right))

    for step in range(half // 2 - 1, 1, -1):
        right = with_block(step, right)
    early_part = pltpu.VMEM((rows_here, 8 * len(strips_of(half, rows_here)[0]), hidden), F32)
    tile_part = pltpu.VMEM((rows_here, half * rows_here, hidden), F32)
    right, own_early = in_vmem(
        *call(functools.partial(near_kernel, half, 1), out_shape=(rights, early_part), input_output_aliases={3: 0})(
            *in_vmem(blocks[1]), w_v, left, *in_vmem(right)
        )
    )
    for step in range(half - 1, half // 2, -1):
        right = with_block(step, right)
    left, far_tile = in_vmem(
        *call(functools.partial(far_kernel, half), out_shape=(lefts, tile_part), input_output_aliases={3: 0})(
            *in_vmem(far), w_v, *in_vmem(right), left
        )
    )
    last, swap = half // 2, [(0, 1), (1, 0)]
    (block,) = in_vmem(blocks[last])
    right, far_tile = in_vmem(
        *call(
            functools.partial(give_kernel, half, last), out_shape=(rights, tile_part), input_output_aliases={3: 0, 4: 1}
        )(block, w_v, left, *in_vmem(right), far_tile)
    )
    got_far = lax.ppermute(far_tile, "col", swap)
    own_pieces = [pltpu.VMEM((p.stop - p.start, *tile_part.shape[1:]), F32) for p in pieces_of(rows_here)]
    left, right, keep, *own_parts = in_vmem(
        *call(
            functools.partial(keep_kernel, half, last),
            out_shape=(lefts, rights, tile_part, tile_part, *own_pieces),
            input_output_aliases={4: 0, 5: 1},
        )(*in_vmem(far), block, w_v, own_early, left, right)
    )
    (tri,) = in_vmem(call(norm_kernel, out_shape=pltpu.VMEM(x.shape, BF16))(keep, *in_vmem(got_far)))
    pairs = [(2 * r, 2 * (r ^ half) + r // half) for r in range(rows)]
    pairs += [(2 * r + 1, 2 * r if r < half else 2 * (r ^ 1) + 1) for r in range(rows)]
    arrived = lax.ppermute(tri, ("row", "col"), pairs)
    own_tile, *pieces = in_vmem(
        *call(
            functools.partial(own_sums_kernel, half),
            out_shape=(tile_part, *own_pieces),
            input_output_aliases={4 + n: n for n in range(1 + PIECES)},
        )(left, right, own_early, tri, *own_parts)
    )
    got_own = [lax.ppermute(piece, "col", swap) for piece in pieces]
    in_place = pl.BlockSpec(memory_space=pltpu.VMEM)
    in_hbm = pl.BlockSpec(memory_space=pltpu.HBM)
    scratch = [pltpu.VMEM(x.shape, BF16), pltpu.SemaphoreType.DMA]
    out = call(
        functools.partial(finish_own_kernel, half),
        in_specs=[in_place] * (3 + PIECES),
        out_specs=in_hbm,
        out_shape=pltpu.HBM(x.shape, BF16),
        scratch_shapes=scratch,
    )(own_tile, *in_vmem(*got_own), gate, o_v)
    return call(
        functools.partial(finish_far_kernel, half),
        in_specs=[in_place] * 3 + [in_hbm],
        out_specs=in_hbm,
        out_shape=pltpu.HBM(x.shape, BF16),
        input_output_aliases={3: 0},
        scratch_shapes=scratch,
    )(*in_vmem(arrived), gate, o_v, pltpu.with_memory_space_constraint(out, pltpu.HBM))


def gather_plan(pair_rep, proj_weight, gate_weight, out_weight):
    rows_here, cols_here, channels = pair_rep.shape
    hidden = out_weight.shape[0]
    normed = layer_norm(pair_rep.astype(F32)).astype(BF16)
    flat_rows = normed.reshape(-1, channels)
    projected = jnp.dot(flat_rows, proj_weight, preferred_element_type=F32)
    left, right = (
        (jax.nn.sigmoid(projected[:, at : at + hidden]) * projected[:, at + hidden : at + 2 * hidden])
        .astype(BF16)
        .reshape(rows_here, cols_here, hidden)
        for at in (0, 2 * hidden)
    )
    gating = jax.nn.sigmoid(jnp.dot(flat_rows, gate_weight, preferred_element_type=F32))
    left_full = lax.all_gather(left, "col", axis=1, tiled=True)
    right_all = lax.all_gather(lax.all_gather(right, "col", axis=1, tiled=True), "row", axis=0, tiled=True)
    mine = lax.dynamic_slice_in_dim(right_all, lax.axis_index("col") * cols_here, cols_here, 0)
    combined = jnp.einsum("ikc,jkc->ijc", left_full, mine, preferred_element_type=F32)
    tri_normed = layer_norm(combined).astype(BF16).reshape(-1, hidden)
    update = jnp.dot(tri_normed, out_weight, preferred_element_type=F32) * gating
    return update.astype(BF16).reshape(rows_here, cols_here, channels)


def solution(mesh):
    def per_device(pair_rep, proj_weight, gate_weight, out_weight):
        rows_here, cols_here, channels = pair_rep.shape
        hidden = out_weight.shape[0]
        rows, cols = mesh.shape["row"], mesh.shape["col"]
        half = rows // 2
        held = 4 * hidden * (half + 3) * rows_here * cols_here + 12 * hidden * half * rows_here**2
        fits = held + 2 * half * pair_rep.size <= VMEM_BUDGET and channels == hidden
        even = cols == 2 and rows >= 4 and rows & (rows - 1) == 0 and half * rows_here == cols_here
        tiled = rows_here * cols_here % 16 == 0 and cols_here % 8 == 0 and channels % 128 == 0
        if fits and even and tiled:
            return fast_plan(mesh, pair_rep, proj_weight, gate_weight, out_weight)
        return gather_plan(pair_rep, proj_weight, gate_weight, out_weight)

    return jax.shard_map(
        per_device,
        mesh=mesh,
        in_specs=(PLACED, P(), P(), P()),
        out_specs=PLACED,
        check_vma=False,
    )
```
